512 devices in a mesh: sib: 2 (over core), row: 16 (over z_lo, y), col: 16 (over x, z_hi).
Axes of the slice: x: 4, y: 8, z: 8 (z_hi: 4, z_lo: 2; z = z_hi * 2 + z_lo), core: 2. Of those that a mesh axis runs over, the one named last changes fastest.
Arguments:
- child_pivot: bfloat16 [2, 384, 384], P('sib'), as said below
- child_border: bfloat16 [2, 12288, 384], P('sib', 'row')
- child_trailing: bfloat16 [2, 12288, 12288], P('sib', 'row', 'col'), as said below
- parent_pivot: bfloat16 [384, 384], replicated, as said below
- child_maps: int32 [2, 96], replicated, may hold values from 0 to 127, as said below
Outputs:
- parent_panel: bfloat16 [16384, 384], P('row')
- parent_update: bfloat16 [16384, 16384], P('row', ('sib', 'col'))
The draws below stay inside these ranges and needn't reach their ends.
Inputs may be any that keep to these rules, and one draw needn't show every extreme that they name: `child_maps`: each row lists 96 different parent blocks in increasing order; every parent block appears in at least one of the two rows. Each child_pivot[s] is symmetric positive definite. Each child_trailing[s] is symmetric, and each child's whole front [[child_pivot[s], child_border[s]^T], [child_border[s], child_trailing[s]]] is positive definite. `parent_pivot`: symmetric positive definite.
All inputs are finite; a program needn't handle non-finite values.
Results may differ from the reference program's by a relative error of at most 0.01.
Values may be sent and summed in bfloat16 or wider, within the bound.
A program may use at most 64 MiB of HBM per device.

```python
import math
import jax
import jax.numpy as jnp
from jax import lax

BLOCK = 128
CU = 12288
CP = 384
PF = 16384
PP = 384
CB = 96
PB = 128


HIGHEST = lax.Precision.HIGHEST


def symmetric_block(sub_key, matrix_order, lower_bound, upper_bound, spread, stretch):
    noise_key, diag_key, scale_key = jax.random.split(sub_key, 3)
    random_part = jax.random.normal(noise_key, (matrix_order, matrix_order), jnp.float32)
    random_part = (random_part + random_part.T) * (spread / math.sqrt(2.0 * matrix_order))
    diagonal = jax.random.uniform(diag_key, (matrix_order,), jnp.float32, lower_bound, upper_bound)
    positions = jnp.arange(matrix_order)
    matrix = random_part + jnp.where(positions[:, None] == positions[None, :], diagonal[:, None], 0.0)
    scales = jnp.exp(jax.random.uniform(scale_key, (matrix_order,), jnp.float32, 0.0, stretch))
    return matrix * scales[:, None] * scales[None, :]


def border_values(base_key, stretch):
    border_key = jax.random.fold_in(base_key, 40)
    value_key, scale_key = jax.random.split(border_key)
    values = jax.random.normal(value_key, (2, CU, CP), jnp.float32) * math.sqrt(10.0 / CP)
    row_scales = jnp.exp(jax.random.uniform(scale_key, (2, CU, 1), jnp.float32, 0.0, stretch))
    return (values * row_scales).astype(jnp.bfloat16)


def draw_child_pivot(key, part):
    key = jax.random.fold_in(key, 1)
    stretch = 0.0
    child_keys = jax.random.split(key, 2)

    def one_child(sub_key):
        return symmetric_block(sub_key, CP, 4.0, 6.0, 1.0, stretch)
    return lax.map(one_child, child_keys).astype(jnp.bfloat16)


def draw_child_trailing(key, part):
    stretch = 0.0
    border_stretch = 0.0
    border = border_values(key, border_stretch).astype(jnp.float32)
    key = jax.random.fold_in(key, 2)
    child_keys = jax.random.split(key, 2)

    def one_child(pair):
        sub_key, border_rows = pair
        base = symmetric_block(sub_key, CU, 4.0, 6.0, 0.8, stretch)
        extra_key = jax.random.fold_in(sub_key, 7)
        extra_rows = jax.random.normal(extra_key, (CU, CP), jnp.float32) * math.sqrt(4.0 / CP)
        factors = jnp.concatenate([border_rows / math.sqrt(1.5), extra_rows], axis=1)
        coupling = jnp.dot(factors, factors.T, precision=HIGHEST, preferred_element_type=jnp.float32)
        return (base + coupling).astype(jnp.bfloat16)
    return lax.map(one_child, (child_keys, border))


def draw_parent_pivot(key, part):
    key = jax.random.fold_in(key, 3)
    stretch = 0.0
    return symmetric_block(key, PP, 4.0, 6.0, 1.0, stretch).astype(jnp.bfloat16)


def draw_child_border(key, part):
    border_stretch = 0.0
    return border_values(key, border_stretch)


def draw_child_maps(key, part):
    key = jax.random.fold_in(key, 5)
    order_key, chosen_key = jax.random.split(key)
    shuffled = jax.random.permutation(order_key, PB).astype(jnp.int32)
    first_map = jnp.sort(shuffled[:CB])
    missing = shuffled[CB:]
    chosen = jax.random.permutation(chosen_key, CB)[:2 * CB - PB]
    second = jnp.sort(jnp.concatenate([missing, shuffled[:CB][chosen]]))
    return jnp.stack([first_map, second]).astype(jnp.int32)


def setup_inputs(seed: int = 0) -> dict:
    splits = jax.random.split(jax.random.key(seed), 6)
    return {
        "child_pivot": draw_child_pivot(jax.random.fold_in(splits[5], 71), 0),
        "child_border": draw_child_border(jax.random.fold_in(splits[5], 71), 0),
        "child_trailing": draw_child_trailing(jax.random.fold_in(splits[5], 71), 0),
        "parent_pivot": draw_parent_pivot(jax.random.fold_in(splits[5], 71), 0),
        "child_maps": draw_child_maps(jax.random.fold_in(splits[5], 71), 0),
    }


def lower_solve(factor, rhs_rows):
    return jax.scipy.linalg.solve_triangular(factor, rhs_rows.T, lower=True).T

def inverse_map(block_map, parent_blocks):
    child_blocks = block_map.shape[0]
    matches = block_map[:, None] == jnp.arange(parent_blocks, dtype=jnp.int32)[None, :]
    found_count = jnp.sum(matches.astype(jnp.int32), axis=0)
    source = jnp.sum(jnp.where(matches, jnp.arange(child_blocks, dtype=jnp.int32)[:, None], 0), axis=0)
    return jnp.where(found_count > 0, source, child_blocks).astype(jnp.int32)

def widen(update, inverse):
    child_blocks = update.shape[0] // BLOCK
    block_tiles = update.reshape(child_blocks, BLOCK, child_blocks, BLOCK)
    block_tiles = jnp.pad(block_tiles, ((0, 1), (0, 0), (0, 1), (0, 0)))
    block_tiles = jnp.take(block_tiles, inverse, axis=0)
    block_tiles = jnp.take(block_tiles, inverse, axis=2)
    return block_tiles.reshape(PF, PF)

def reference(child_pivot, child_border, child_trailing, parent_pivot, child_maps):
    front_full = jnp.zeros((PF, PF), jnp.float32)
    for child_index in range(2):
        factor = jnp.linalg.cholesky(child_pivot[child_index].astype(jnp.float32))
        panel_rows = lower_solve(factor, child_border[child_index].astype(jnp.float32))
        panel_short = panel_rows.astype(jnp.bfloat16)
        schur_part = child_trailing[child_index].astype(jnp.float32) - jnp.dot(panel_short.astype(jnp.float32), panel_short.T.astype(jnp.float32), preferred_element_type=jnp.float32)
        update = schur_part.astype(jnp.bfloat16)
        inverse = inverse_map(child_maps[child_index], PF // BLOCK)
        front_full = front_full + widen(update, inverse).astype(jnp.float32)
    front_full = front_full.at[:PP, :PP].add(parent_pivot.astype(jnp.float32))
    parent_factor = jnp.linalg.cholesky(front_full[:PP, :PP])
    pivot_panel = lower_solve(parent_factor, front_full[:, :PP])
    panel_short = pivot_panel.astype(jnp.bfloat16)
    schur_part = front_full - jnp.dot(panel_short.astype(jnp.float32), panel_short.T.astype(jnp.float32), preferred_element_type=jnp.float32)
    positions = jnp.arange(PF)
    retained = (positions >= PP)[:, None] & (positions >= PP)[None, :]
    parent_update = jnp.where(retained, schur_part, 0.0).astype(jnp.bfloat16)
    return (panel_short, parent_update)
```

```python
import jax
import jax.numpy as jnp
from jax import lax
from jax.experimental import pallas as pl
from jax.experimental.pallas import tpu as pltpu
from jax.sharding import PartitionSpec as P

BF16 = jnp.bfloat16
F32 = jnp.float32
HIGHEST = lax.Precision.HIGHEST
NT = (((1,), (1,)), ((), ()))
MESH = pl.DeviceIdType.MESH
ROWS = 16
COLS = 16


def mm(a, b):
    return jnp.dot(a, b, precision=HIGHEST, preferred_element_type=F32)


def mm_nt(a, b):
    return lax.dot_general(a, b, NT, precision=HIGHEST, preferred_element_type=F32)


def dot_nt(a, b):
    return lax.dot_general(a, b, NT, preferred_element_type=F32)


def block_inverse(s_ref, i_ref):
    n = 128
    rows = lax.broadcasted_iota(jnp.int32, (n, n), 0)
    cols = lax.broadcasted_iota(jnp.int32, (n, n), 1)
    x = s_ref[...]
    m = jnp.where(rows == cols, 1.0, 0.0)
    for panel in range(n // 8):
        for o in range(0, 8, 4):
            j = 8 * panel + o
            w = [jnp.broadcast_to(x[:, j + k:j + k + 1], x.shape) for k in range(4)]
            g = [[w[q][o + p:o + p + 1, :] for q in range(4)] for p in range(4)]
            xr = [x[o + k:o + k + 1, :] for k in range(4)]
            mr = [m[o + k:o + k + 1, :] for k in range(4)]
            a, b, c = g[0][0], g[1][0], g[1][1]
            inv = 1.0 / (a * c - b * b)
            ci, bi, ai = c * inv, b * inv, a * inv
            def pair(r1, r2, ci=ci, bi=bi, ai=ai):
                return ci * r1 - bi * r2, ai * r2 - bi * r1
            x1p, x2p = pair(xr[0], xr[1])
            m1p, m2p = pair(mr[0], mr[1])
            i_ref[j:j + 1, :] = mr[0] * lax.rsqrt(a)
            i_ref[j + 1:j + 2, :] = m2p * lax.rsqrt(ai)
            p20, p21 = pair(g[2][0], g[2][1])
            p30, p31 = pair(g[3][0], g[3][1])
            a2 = g[2][2] - (g[2][0] * p20 + g[2][1] * p21)
            b2 = g[3][2] - (g[3][0] * p20 + g[3][1] * p21)
            c2 = g[3][3] - (g[3][0] * p30 + g[3][1] * p31)
            inv2 = 1.0 / (a2 * c2 - b2 * b2)
            ci2, bi2, ai2 = c2 * inv2, b2 * inv2, a2 * inv2
            x3 = xr[2] - g[2][0] * x1p - g[2][1] * x2p
            x4 = xr[3] - g[3][0] * x1p - g[3][1] * x2p
            m3 = mr[2] - g[2][0] * m1p - g[2][1] * m2p
            m4 = mr[3] - g[3][0] * m1p - g[3][1] * m2p
            x3p, x4p = pair(x3, x4, ci2, bi2, ai2)
            m3p, m4p = pair(m3, m4, ci2, bi2, ai2)
            i_ref[j + 2:j + 3, :] = m3 * lax.rsqrt(a2)
            i_ref[j + 3:j + 4, :] = m4p * lax.rsqrt(ai2)
            if o == 4:
                x, m = x[8:, :], m[8:, :]
                w = [t[8:, :] for t in w]
                if panel == n // 8 - 1:
                    break
            f1, f2 = pair(w[0], w[1])
            u3 = w[2] - f1 * g[2][0] - f2 * g[2][1]
            u4 = w[3] - f1 * g[3][0] - f2 * g[3][1]
            x = x - w[0] * x1p - w[1] * x2p - u3 * x3p - u4 * x4p
            m = m - w[0] * m1p - w[1] * m2p - u3 * m3p - u4 * m4p


def factor_inverse(a_ref, out_ref, s_ref, i_ref, l_ref):
    n = 384
    a = a_ref[...]
    rows = lax.broadcasted_iota(jnp.int32, (n, n), 0)
    cols = lax.broadcasted_iota(jnp.int32, (n, n), 1)
    diag = jnp.where(rows == cols, a, 0.0)
    dr = lax.rsqrt(jnp.sum(diag, axis=0, keepdims=True))
    dc = lax.rsqrt(jnp.sum(diag, axis=1, keepdims=True))
    a_ref[...] = a * dr * dc
    b = [pl.ds(128 * k, 128) for k in range(3)]
    out_ref[...] = jnp.zeros((n, n), F32)
    s_ref[...] = a_ref[b[0], b[0]]

    def body(k, carry):
        block_inverse(s_ref, i_ref)
        inv = i_ref[...]

        @pl.when(k == 0)
        def _():
            out_ref[b[0], b[0]] = inv
            l21 = mm_nt(a_ref[b[1], b[0]], inv)
            s_ref[...] = a_ref[b[1], b[1]] - mm_nt(l21, l21)
            l31 = mm_nt(a_ref[b[2], b[0]], inv)
            a_ref[b[2], b[1]] = a_ref[b[2], b[1]] - mm_nt(l31, l21)
            a_ref[b[2], b[2]] = a_ref[b[2], b[2]] - mm_nt(l31, l31)
            l_ref[0] = mm(l21, inv)
            l_ref[1] = mm(l31, inv)

        @pl.when(k == 1)
        def _():
            out_ref[b[1], b[1]] = inv
            l32 = mm_nt(a_ref[b[2], b[1]], inv)
            s_ref[...] = a_ref[b[2], b[2]] - mm_nt(l32, l32)
            x21 = -mm(inv, l_ref[0])
            out_ref[b[1], b[0]] = x21
            l_ref[1] = l_ref[1] + mm(l32, x21)
            l_ref[2] = mm(l32, inv)

        @pl.when(k == 2)
        def _():
            out_ref[b[2], b[2]] = inv
            out_ref[b[2], b[0]] = -mm(inv, l_ref[1])
            out_ref[b[2], b[1]] = -mm(inv, l_ref[2])

        return carry

    lax.fori_loop(0, 3, body, 0)
    out_ref[...] = out_ref[...] * dr


FACTOR_SCRATCH = [
    pltpu.VMEM((384, 384), F32),
    pltpu.VMEM((128, 128), F32),
    pltpu.VMEM((128, 128), F32),
    pltpu.VMEM((3, 128, 128), F32),
]


def child_kernel(pivot_ref, out_ref, a_ref, s_ref, i_ref, l_ref):
    a_ref[...] = pivot_ref[...].astype(F32)
    factor_inverse(a_ref, out_ref, s_ref, i_ref, l_ref)


def child_inverse(pivot):
    return pl.pallas_call(
        child_kernel,
        out_shape=jax.ShapeDtypeStruct((384, 384), F32),
        in_specs=[pl.BlockSpec(memory_space=pltpu.VMEM)],
        out_specs=pl.BlockSpec(memory_space=pltpu.VMEM),
        scratch_shapes=FACTOR_SCRATCH,
        compiler_params=pltpu.CompilerParams(vmem_limit_bytes=32 << 20),
        cost_estimate=pl.CostEstimate(flops=2 * 10**9, bytes_accessed=10**6, transcendentals=0),
    )(pivot)


def panel_of(border, inverse):
    high = inverse.astype(BF16)
    rest = inverse - high.astype(F32)
    middle = rest.astype(BF16)
    low = (rest - middle.astype(F32)).astype(BF16)
    return (dot_nt(border, high) + (dot_nt(border, middle) + dot_nt(border, low))).astype(BF16)


def front_kernel(
    maps_ref, trailing_ref, border_ref, cross_ref, inverse_ref, pivot_ref,
    panel_ref, update_ref,
    pr, pc, u, z1, w1, v, z3, xs, xr, fs, fr, y, z4, prow, pcol, crn, parent_inv,
    a_ref, s_ref, i_ref, l_ref,
    z1s, z1r, z2s, z2r, z3s, z3r, z4s, z4r, g1s, g1r, g2s, g2r,
    cas, car, cbs, cbr, ccs, ccr, sws, swr, xss, xsr, lsem,
):
    s = lax.axis_index("sib")
    r = lax.axis_index("row")
    c = lax.axis_index("col")
    other = 1 - s
    g, h = r // 2, r % 2

    sends_cols = s == r // 8
    cols_to = 2 * (r % 8) + c // 8
    cols_from_row = 8 * s + c // 2
    cols_from_col = 8 * (c % 2)

    def remote(src, dst, send, recv, **to):
        return pltpu.make_async_remote_copy(
            src_ref=src, dst_ref=dst, send_sem=send, recv_sem=recv, device_id=to, device_id_type=MESH
        )

    def each(first, last, body):
        def step(k, carry):
            body(k)
            return carry
        lax.fori_loop(first, last, step, 0)

    barrier = pltpu.get_barrier_semaphore()

    def greet(j):
        pl.semaphore_signal(barrier, inc=1, device_id={"row": lax.rem(r + j, ROWS)}, device_id_type=MESH)
        pl.semaphore_signal(barrier, inc=1, device_id={"col": lax.rem(c + j, COLS)}, device_id_type=MESH)

    each(1, 16, greet)
    pl.semaphore_signal(barrier, inc=1, device_id={"sib": other}, device_id_type=MESH)

    def greet_cols(k):
        @pl.when(jnp.logical_not((cols_from_row == r) & (cols_from_col + k == c)))
        def _():
            pl.semaphore_signal(
                barrier, inc=1, device_id={"row": cols_from_row, "col": cols_from_col + k}, device_id_type=MESH
            )

    each(0, 8, greet_cols)

    inverse = inverse_ref[...]
    pr[...] = panel_of(border_ref[...], inverse)
    pc[...] = panel_of(cross_ref[...], inverse)
    for i in range(6):
        rows = pl.ds(128 * i, 128)
        value = trailing_ref[rows, :].astype(F32) - dot_nt(pr[rows, :], pc[...])
        value = value.astype(BF16)
        for q in range(6):
            u[q, i] = value[:, 128 * q:128 * (q + 1)].reshape(8, 16, 128)

    expected = 31 + jnp.where(sends_cols, 16 - (cols_to == c).astype(jnp.int32), 0)
    pl.semaphore_wait(barrier, expected)

    at_root = (r == 0) & (c == 0)
    holds = r < 8

    def corner_a(k):
        return remote(u.at[0:3, 0:3, k], crn.at[s, :, :, k], cas.at[k], car.at[0], row=k)

    @pl.when(at_root)
    def _():
        each(1, 8, lambda k: corner_a(k).start())
        own = pltpu.make_async_copy(u.at[0:3, 0:3, 0], crn.at[s, :, :, 0], lsem.at[0])
        own.start()
        own.wait()

    def first(k):
        return remote(
            u.at[pl.ds(3 * (k % 2), 3), :, k // 2], z1.at[:, pl.ds(6 * r, 6)], z1s.at[k], z1r.at[r], row=k
        )

    def first_from(k):
        return remote(
            u.at[pl.ds(3 * h, 3), :, g], z1.at[:, pl.ds(6 * k, 6)], z1s.at[k], z1r.at[k], row=k
        )

    each(1, 16, lambda j: first(lax.rem(r + j, ROWS)).start())
    own1 = pltpu.make_async_copy(u.at[pl.ds(3 * h, 3), :, g], z1.at[:, pl.ds(6 * r, 6)], lsem.at[1])
    own1.start()
    z1[:, 96] = jnp.zeros((3, 16, 128), BF16)
    z3[96] = jnp.zeros((4, 16, 128), BF16)
    own1.wait()

    def corner_b(k):
        return remote(crn.at[s, :, :, r], crn.at[s, :, :, r], cbs.at[k], cbr.at[0], col=k)

    @pl.when(holds & (c == 0))
    def _():
        @pl.when(r > 0)
        def _():
            corner_a(r).wait_recv()
        each(1, 16, lambda k: corner_b(k).start())

    each(1, 16, lambda j: first_from(lax.rem(r + j, ROWS)).wait_recv())

    def second(k):
        return remote(
            w1.at[:, pl.ds(8 * k, 8)], v.at[pl.ds(3 * h, 3), :, g], z2s.at[k], z2r.at[r], row=k
        )

    def second_from(k):
        return remote(
            w1.at[:, pl.ds(8 * r, 8)], v.at[pl.ds(3 * (k % 2), 3), :, k // 2], z2s.at[k], z2r.at[k], row=k
        )

    def widen_rows(k):
        for j in range(8):
            p = 8 * k + j
            w1[:, p] = z1[:, maps_ref[s, p]]

    def send_second(j):
        k = lax.rem(r + j, ROWS)
        widen_rows(k)
        second(k).start()

    each(1, 16, send_second)
    widen_rows(r)
    own2 = pltpu.make_async_copy(w1.at[:, pl.ds(8 * r, 8)], v.at[pl.ds(3 * h, 3), :, g], lsem.at[2])
    own2.start()

    def corner_c(k):
        return remote(crn.at[s, :, :, r], crn.at[s, :, :, r], ccs.at[k], ccr.at[r], row=k)

    def corner_c_from(k):
        return remote(crn.at[s, :, :, k], crn.at[s, :, :, k], ccs.at[k], ccr.at[k], row=k)

    @pl.when(holds)
    def _():
        @pl.when(c > 0)
        def _():
            corner_b(c).wait_recv()
        each(1, 16, lambda j: corner_c(lax.rem(r + j, ROWS)).start())

    own2.wait()
    each(1, 16, lambda j: second_from(lax.rem(r + j, ROWS)).wait_recv())

    def third(k):
        return remote(
            v.at[:, k // 2, pl.ds(4 * (k % 2), 4)], z3.at[pl.ds(6 * c, 6)], z3s.at[k], z3r.at[c], col=k
        )

    def third_from(k):
        return remote(
            v.at[:, c // 2, pl.ds(4 * (c % 2), 4)], z3.at[pl.ds(6 * k, 6)], z3s.at[k], z3r.at[k], col=k
        )
    each(1, 16, lambda j: third(lax.rem(c + j, COLS)).start())
    own3 = pltpu.make_async_copy(
        v.at[:, c // 2, pl.ds(4 * (c % 2), 4)], z3.at[pl.ds(6 * c, 6)], lsem.at[3]
    )
    own3.start()

    def corner_rest(k):
        @pl.when(k != r)
        def _():
            corner_c_from(k).wait_recv()

    each(0, 8, corner_rest)
    swap = remote(crn.at[s], crn.at[s], sws.at[0], swr.at[0], sib=other)
    swap_back = remote(crn.at[s], crn.at[other], sws.at[0], swr.at[0], sib=other)
    swap.start()
    swap_back.wait_recv()
    for p in range(3):
        for q in range(3):
            total = pivot_ref[128 * p:128 * (p + 1), 128 * q:128 * (q + 1)].astype(F32)
            for child in range(2):
                i, j = maps_ref[child, p], maps_ref[child, q]
                present = (i < 3) & (j < 3)
                block = crn[child, jnp.minimum(j, 2), jnp.minimum(i, 2)].astype(F32).reshape(128, 128)
                total = total + jnp.where(present, block, 0.0)
            a_ref[128 * p:128 * (p + 1), 128 * q:128 * (q + 1)] = total
    factor_inverse(a_ref, parent_inv, s_ref, i_ref, l_ref)

    own3.wait()
    each(1, 16, lambda j: third_from(lax.rem(c + j, COLS)).wait_recv())

    def strip(p):
        return z3[maps_ref[s, p]]

    for p in range(3):
        fs[p] = strip(p)
    swap_pivots = remote(fs, fr, sws.at[1], swr.at[1], sib=other)
    swap_pivots.start()

    def half(k):
        return remote(xs.at[pl.ds(4 * k, 4)], xr.at[pl.ds(4 * k, 4)], xss.at[k], xsr.at[k], sib=other)

    def send_half(j):
        k = lax.rem(c + j, COLS)
        for q in range(4):
            xs[4 * k + q] = strip(64 * other + 4 * k + q)
        half(k).start()

    each(1, 17, send_half)

    swap_pivots.wait_recv()
    first_rows = (r == 0) & (c < 6)
    start_row = pl.multiple_of(64 * jnp.minimum(c, 5), 64)
    anchor = jnp.where(first_rows, pivot_ref[pl.ds(start_row, 64), :].astype(F32), 0.0)
    rows = jnp.concatenate(
        [fs[p].astype(F32).reshape(64, 128) + fr[p].astype(F32).reshape(64, 128) for p in range(3)], axis=1
    )
    piece = mm_nt(rows + anchor, parent_inv[...]).astype(BF16)
    prow[c] = piece

    def gather_rows(k):
        return remote(prow.at[c], prow.at[c], g1s.at[k], g1r.at[c], col=k)

    def gather_rows_from(k):
        return remote(prow.at[c], prow.at[k], g1s.at[k], g1r.at[k], col=k)

    def gather_cols(k):
        return remote(prow.at[c], pcol.at[c % 8], g2s.at[k], g2r.at[c % 8], row=k, col=cols_to)

    def gather_cols_from(k):
        return remote(
            prow.at[c], pcol.at[k], g2s.at[k], g2r.at[k], row=cols_from_row, col=cols_from_col + k
        )

    def is_other(k):
        return jnp.logical_not((k == r) & (cols_to == c))

    @pl.when(sends_cols)
    def _():
        def go(j):
            k = lax.rem(r + j, ROWS)

            @pl.when(is_other(k))
            def _():
                gather_cols(k).start()

            @pl.when(jnp.logical_not(is_other(k)))
            def _():
                pcol[c % 8] = piece

        each(1, 17, go)

    each(1, 16, lambda j: gather_rows(lax.rem(c + j, COLS)).start())

    def fourth(k):
        return remote(y.at[pl.ds(4 * k, 4)], z4.at[c], z4s.at[k], z4r.at[c], col=k)

    def fourth_from(k):
        return remote(y.at[pl.ds(4 * k, 4)], z4.at[k], z4s.at[k], z4r.at[k], col=k)

    def both(k, q):
        return (strip(64 * s + 4 * k + q).astype(F32) + xr[4 * k + q].astype(F32)).astype(BF16)

    def send_fourth(j):
        k = lax.rem(c + j, COLS)
        half(k).wait_recv()
        for q in range(4):
            y[4 * k + q] = both(k, q)
        fourth(k).start()

    each(1, 16, send_fourth)
    half(c).wait_recv()
    for q in range(4):
        z4[c, q] = both(c, q)

    def cols_rest(k):
        @pl.when(jnp.logical_not((cols_from_row == r) & (cols_from_col + k == c)))
        def _():
            gather_cols_from(k).wait_recv()

    each(0, 8, cols_rest)
    for chunk in range(4):
        def rows_rest(k):
            @pl.when(k != c)
            def _():
                gather_rows_from(k).wait_recv()
                fourth_from(k).wait_recv()

        each(4 * chunk, 4 * chunk + 4, rows_rest)
        left = prow[4 * chunk:4 * chunk + 4].reshape(256, 384)
        panel_ref[256 * chunk:256 * (chunk + 1), :] = left
        row_ids = 1024 * r + 256 * chunk + lax.broadcasted_iota(jnp.int32, (256, 128), 0)
        for q in range(4):
            right = pcol[2 * q:2 * q + 2].reshape(128, 384)
            front = z4[4 * chunk:4 * chunk + 4, q].astype(F32).reshape(256, 128)
            value = front - dot_nt(left, right)
            col_ids = 512 * (16 * s + c) + 128 * q + lax.broadcasted_iota(jnp.int32, (256, 128), 1)
            value = jnp.where((row_ids >= 384) & (col_ids >= 384), value, 0.0)
            update_ref[256 * chunk:256 * (chunk + 1), 128 * q:128 * (q + 1)] = value.astype(BF16)

    @pl.when(at_root)
    def _():
        each(1, 8, lambda k: corner_a(k).wait_send())

    @pl.when(holds & (c == 0))
    def _():
        each(1, 16, lambda k: corner_b(k).wait_send())

    @pl.when(holds)
    def _():
        each(1, 16, lambda j: corner_c(lax.rem(r + j, ROWS)).wait_send())

    @pl.when(sends_cols)
    def _():
        def gone(k):
            @pl.when(is_other(k))
            def _():
                gather_cols(k).wait_send()

        each(0, 16, gone)

    def all_gone(j):
        k = lax.rem(r + j, ROWS)
        first(k).wait_send()
        second(k).wait_send()
        k = lax.rem(c + j, COLS)
        third(k).wait_send()
        fourth(k).wait_send()
        gather_rows(k).wait_send()

    each(1, 16, all_gone)
    each(0, 16, lambda k: half(k).wait_send())
    swap.wait_send()
    swap_pivots.wait_send()


def front_step(maps, trailing, border, cross, inverse, pivot):
    vmem = pl.BlockSpec(memory_space=pltpu.VMEM)
    dma = pltpu.SemaphoreType.DMA
    buffers = [
        (768, 384), (768, 384),
        (6, 6, 8, 16, 128),
        (3, 97, 16, 128),
        (3, 128, 16, 128),
        (6, 8, 8, 16, 128),
        (97, 4, 16, 128),
        (64, 4, 16, 128), (64, 4, 16, 128),
        (3, 4, 16, 128), (3, 4, 16, 128),
        (64, 4, 16, 128),
        (16, 4, 4, 16, 128),
        (16, 64, 384), (8, 64, 384),
        (2, 3, 3, 8, 16, 128),
    ]
    counts = [16] * 12 + [8, 1, 16, 1, 16, 8, 2, 2, 16, 16, 4]
    return pl.pallas_call(
        front_kernel,
        out_shape=(
            jax.ShapeDtypeStruct((1024, 384), BF16),
            jax.ShapeDtypeStruct((1024, 512), BF16),
        ),
        in_specs=[pl.BlockSpec(memory_space=pltpu.SMEM)] + [vmem] * 5,
        out_specs=(vmem, vmem),
        scratch_shapes=[pltpu.VMEM(shape, BF16) for shape in buffers]
        + [pltpu.VMEM((384, 384), F32)]
        + FACTOR_SCRATCH
        + [dma((count,)) for count in counts],
        compiler_params=pltpu.CompilerParams(
            collective_id=0, has_side_effects=True, vmem_limit_bytes=50 << 20
        ),
        cost_estimate=pl.CostEstimate(flops=10**10, bytes_accessed=10**8, transcendentals=0),
    )(maps, trailing, border, cross, inverse, pivot)


def inverse_maps(child_maps):
    matches = child_maps[:, :, None] == jnp.arange(128, dtype=jnp.int32)
    source = jnp.arange(96, dtype=jnp.int32)[None, :, None]
    return jnp.min(jnp.where(matches, source, 96), axis=1).astype(jnp.int32)


def shards(child_pivot, child_border, child_trailing, parent_pivot, child_maps):
    across = [(16 * i + j, 16 * j + i) for i in range(ROWS) for j in range(COLS)]
    cross = lax.ppermute(child_border[0], ("row", "col"), across)
    inverse = child_inverse(child_pivot[0])
    return front_step(
        inverse_maps(child_maps), child_trailing[0], child_border[0], cross, inverse, parent_pivot
    )


def solution(mesh):
    placed = (P("sib", None, None), P("sib", "row", None), P("sib", "row", "col"), P(), P())
    return jax.shard_map(
        shards,
        mesh=mesh,
        in_specs=placed,
        out_specs=(P("row", None), P("row", ("sib", "col"))),
        check_vma=False,
    )
```

```python
import jax
import jax.numpy as jnp
from jax import lax
from jax.experimental import pallas as pl
from jax.experimental.pallas import tpu as pltpu
from jax.sharding import PartitionSpec as P

BF16 = jnp.bfloat16
F32 = jnp.float32
HIGHEST = lax.Precision.HIGHEST
NT = (((1,), (1,)), ((), ()))
MESH = pl.DeviceIdType.MESH
ROWS = 16
COLS = 16


def mm(a, b):
    return jnp.dot(a, b, precision=HIGHEST, preferred_element_type=F32)


def mm_nt(a, b):
    return lax.dot_general(a, b, NT, precision=HIGHEST, preferred_element_type=F32)


def dot_nt(a, b):
    return lax.dot_general(a, b, NT, preferred_element_type=F32)


def block_inverse(s_ref, i_ref):
    n = 128
    rows = lax.broadcasted_iota(jnp.int32, (n, n), 0)
    cols = lax.broadcasted_iota(jnp.int32, (n, n), 1)
    x = s_ref[...]
    m = jnp.where(rows == cols, 1.0, 0.0)
    for panel in range(n // 8):
        for o in range(0, 8, 4):
            j = 8 * panel + o
            w = [jnp.broadcast_to(x[:, j + k:j + k + 1], x.shape) for k in range(4)]
            g = [[w[q][o + p:o + p + 1, :] for q in range(4)] for p in range(4)]
            xr = [x[o + k:o + k + 1, :] for k in range(4)]
            mr = [m[o + k:o + k + 1, :] for k in range(4)]
            a, b, c = g[0][0], g[1][0], g[1][1]
            inv = 1.0 / (a * c - b * b)
            ci, bi, ai = c * inv, b * inv, a * inv
            def pair(r1, r2, ci=ci, bi=bi, ai=ai):
                return ci * r1 - bi * r2, ai * r2 - bi * r1
            x1p, x2p = pair(xr[0], xr[1])
            m1p, m2p = pair(mr[0], mr[1])
            i_ref[j:j + 1, :] = mr[0] * lax.rsqrt(a)
            i_ref[j + 1:j + 2, :] = m2p * lax.rsqrt(ai)
            p20, p21 = pair(g[2][0], g[2][1])
            p30, p31 = pair(g[3][0], g[3][1])
            a2 = g[2][2] - (g[2][0] * p20 + g[2][1] * p21)
            b2 = g[3][2] - (g[3][0] * p20 + g[3][1] * p21)
            c2 = g[3][3] - (g[3][0] * p30 + g[3][1] * p31)
            inv2 = 1.0 / (a2 * c2 - b2 * b2)
            ci2, bi2, ai2 = c2 * inv2, b2 * inv2, a2 * inv2
            x3 = xr[2] - g[2][0] * x1p - g[2][1] * x2p
            x4 = xr[3] - g[3][0] * x1p - g[3][1] * x2p
            m3 = mr[2] - g[2][0] * m1p - g[2][1] * m2p
            m4 = mr[3] - g[3][0] * m1p - g[3][1] * m2p
            x3p, x4p = pair(x3, x4, ci2, bi2, ai2)
            m3p, m4p = pair(m3, m4, ci2, bi2, ai2)
            i_ref[j + 2:j + 3, :] = m3 * lax.rsqrt(a2)
            i_ref[j + 3:j + 4, :] = m4p * lax.rsqrt(ai2)
            if o == 4:
                x, m = x[8:, :], m[8:, :]
                w = [t[8:, :] for t in w]
                if panel == n // 8 - 1:
                    break
            f1, f2 = pair(w[0], w[1])
            u3 = w[2] - f1 * g[2][0] - f2 * g[2][1]
            u4 = w[3] - f1 * g[3][0] - f2 * g[3][1]
            x = x - w[0] * x1p - w[1] * x2p - u3 * x3p - u4 * x4p
            m = m - w[0] * m1p - w[1] * m2p - u3 * m3p - u4 * m4p


def factor_inverse(a_ref, out_ref, s_ref, i_ref, l_ref, between=None):
    n = 384
    a = a_ref[...]
    rows = lax.broadcasted_iota(jnp.int32, (n, n), 0)
    cols = lax.broadcasted_iota(jnp.int32, (n, n), 1)
    diag = jnp.where(rows == cols, a, 0.0)
    dr = lax.rsqrt(jnp.sum(diag, axis=0, keepdims=True))
    dc = lax.rsqrt(jnp.sum(diag, axis=1, keepdims=True))
    a_ref[...] = a * dr * dc
    b = [pl.ds(128 * k, 128) for k in range(3)]
    out_ref[...] = jnp.zeros((n, n), F32)
    s_ref[...] = a_ref[b[0], b[0]]

    def body(k, carry):
        block_inverse(s_ref, i_ref)
        inv = i_ref[...]

        @pl.when(k == 0)
        def _():
            out_ref[b[0], b[0]] = inv
            l21 = mm_nt(a_ref[b[1], b[0]], inv)
            s_ref[...] = a_ref[b[1], b[1]] - mm_nt(l21, l21)
            l31 = mm_nt(a_ref[b[2], b[0]], inv)
            a_ref[b[2], b[1]] = a_ref[b[2], b[1]] - mm_nt(l31, l21)
            a_ref[b[2], b[2]] = a_ref[b[2], b[2]] - mm_nt(l31, l31)
            l_ref[0] = mm(l21, inv)
            l_ref[1] = mm(l31, inv)
            if between is not None:
                between()

        @pl.when(k == 1)
        def _():
            out_ref[b[1], b[1]] = inv
            l32 = mm_nt(a_ref[b[2], b[1]], inv)
            s_ref[...] = a_ref[b[2], b[2]] - mm_nt(l32, l32)
            x21 = -mm(inv, l_ref[0])
            out_ref[b[1], b[0]] = x21
            l_ref[1] = l_ref[1] + mm(l32, x21)
            l_ref[2] = mm(l32, inv)

        @pl.when(k == 2)
        def _():
            out_ref[b[2], b[2]] = inv
            out_ref[b[2], b[0]] = -mm(inv, l_ref[1])
            out_ref[b[2], b[1]] = -mm(inv, l_ref[2])

        return carry

    lax.fori_loop(0, 3, body, 0)
    out_ref[...] = out_ref[...] * dr


FACTOR_SCRATCH = [
    pltpu.VMEM((384, 384), F32),
    pltpu.VMEM((128, 128), F32),
    pltpu.VMEM((128, 128), F32),
    pltpu.VMEM((3, 128, 128), F32),
]


def panel_of(border, inverse):
    high = inverse.astype(BF16)
    rest = inverse - high.astype(F32)
    middle = rest.astype(BF16)
    low = (rest - middle.astype(F32)).astype(BF16)
    return (dot_nt(border, high) + (dot_nt(border, middle) + dot_nt(border, low))).astype(BF16)


def front_kernel(
    maps_ref, trailing_ref, border_ref, child_ref, pivot_ref,
    panel_ref, update_ref,
    bx, pr, pc, u, z1, w1, v, z3, xs, xr, fs, fr, y, z4, prow, pcol, crn, parent_inv,
    a_ref, s_ref, i_ref, l_ref,
    b1s, b1r, b2s, b2r, z1s, z1r, z2s, z2r, z3s, z3r, z4s, z4r, g1s, g1r, g2s, g2r,
    cas, car, cbs, cbr, ccs, ccr, sws, swr, xss, xsr, hs, hr, lsem,
):
    s = lax.axis_index("sib")
    r = lax.axis_index("row")
    c = lax.axis_index("col")
    other = 1 - s
    g, h = r // 2, r % 2

    sends_cols = s == r // 8
    cols_to = 2 * (r % 8) + c // 8
    cols_from_row = 8 * s + c // 2
    cols_from_col = 8 * (c % 2)

    def remote(src, dst, send, recv, **to):
        return pltpu.make_async_remote_copy(
            src_ref=src, dst_ref=dst, send_sem=send, recv_sem=recv, device_id=to, device_id_type=MESH
        )

    def each(first, last, body):
        def step(k, carry):
            body(k)
            return carry
        lax.fori_loop(first, last, step, 0)

    barrier = pltpu.get_barrier_semaphore()

    def greet(j):
        pl.semaphore_signal(barrier, inc=1, device_id={"row": lax.rem(r + j, ROWS)}, device_id_type=MESH)
        pl.semaphore_signal(barrier, inc=1, device_id={"col": lax.rem(c + j, COLS)}, device_id_type=MESH)

    each(1, 16, greet)
    pl.semaphore_signal(barrier, inc=1, device_id={"sib": other}, device_id_type=MESH)

    def greet_cols(k):
        @pl.when(jnp.logical_not((cols_from_row == r) & (cols_from_col + k == c)))
        def _():
            pl.semaphore_signal(
                barrier, inc=1, device_id={"row": cols_from_row, "col": cols_from_col + k}, device_id_type=MESH
            )

    each(0, 8, greet_cols)

    expected = 31 + jnp.where(sends_cols, 16 - (cols_to == c).astype(jnp.int32), 0)
    pl.semaphore_wait(barrier, expected)

    is_root = r == c

    def scatter(k):
        return remote(border_ref.at[k], bx.at[k], b1s.at[k], b1r.at[0], row=k)

    def scatter_here():
        return remote(border_ref.at[r], bx.at[r], b1s.at[r], b1r.at[0], row=c)

    def spread(k):
        return remote(bx.at[r], bx.at[r], b2s.at[k], b2r.at[r], row=k)

    def spread_from(k):
        return remote(bx.at[r], bx.at[k], b2s.at[k], b2r.at[k], row=k)

    def to_others(body):
        def go(j):
            k = lax.rem(r + j, ROWS)

            @pl.when(k != c)
            def _():
                body(k)

        each(1, 16, go)

    own_border = pltpu.make_async_copy(border_ref, bx, lsem.at[4])

    @pl.when(is_root)
    def _():
        each(1, 16, lambda j: scatter(lax.rem(r + j, ROWS)).start())
        own_border.start()
        own_border.wait()

    def spread_border():
        @pl.when(jnp.logical_not(is_root))
        def _():
            scatter_here().wait_recv()

        to_others(lambda k: spread(k).start())

    a_ref[...] = child_ref[...].astype(F32)
    factor_inverse(a_ref, parent_inv, s_ref, i_ref, l_ref, spread_border)
    inverse = parent_inv[...]
    pr[...] = panel_of(border_ref[...].reshape(768, 384), inverse)

    @pl.when(jnp.logical_not(is_root))
    def _():
        each(1, 16, lambda j: spread_from(lax.rem(r + j, ROWS)).wait_recv())

    pc[...] = panel_of(bx[...].reshape(768, 384), inverse)
    for i in range(6):
        rows = pl.ds(128 * i, 128)
        value = trailing_ref[rows, :].astype(F32) - dot_nt(pr[rows, :], pc[...])
        value = value.astype(BF16)
        for q in range(6):
            u[q, i] = value[:, 128 * q:128 * (q + 1)].reshape(8, 16, 128)

    at_root = (r == 0) & (c == 0)
    holds = r < 8

    def corner_a(k):
        return remote(u.at[0:3, 0:3, k], crn.at[s, :, :, k], cas.at[k], car.at[0], row=k)

    @pl.when(at_root)
    def _():
        each(1, 8, lambda k: corner_a(k).start())
        own = pltpu.make_async_copy(u.at[0:3, 0:3, 0], crn.at[s, :, :, 0], lsem.at[0])
        own.start()
        own.wait()

    def first(k):
        return remote(
            u.at[pl.ds(3 * (k % 2), 3), :, k // 2], z1.at[:, pl.ds(6 * r, 6)], z1s.at[k], z1r.at[r], row=k
        )

    def first_from(k):
        return remote(
            u.at[pl.ds(3 * h, 3), :, g], z1.at[:, pl.ds(6 * k, 6)], z1s.at[k], z1r.at[k], row=k
        )

    each(1, 16, lambda j: first(lax.rem(r + j, ROWS)).start())
    own1 = pltpu.make_async_copy(u.at[pl.ds(3 * h, 3), :, g], z1.at[:, pl.ds(6 * r, 6)], lsem.at[1])
    own1.start()
    z1[:, 96] = jnp.zeros((3, 16, 128), BF16)
    z3[96] = jnp.zeros((4, 16, 128), BF16)
    own1.wait()

    def corner_b(k):
        return remote(crn.at[s, :, :, r], crn.at[s, :, :, r], cbs.at[k], cbr.at[0], col=k)

    @pl.when(holds & (c == 0))
    def _():
        @pl.when(r > 0)
        def _():
            corner_a(r).wait_recv()
        each(1, 16, lambda k: corner_b(k).start())

    each(1, 16, lambda j: first_from(lax.rem(r + j, ROWS)).wait_recv())

    def second(k):
        return remote(
            w1.at[:, pl.ds(8 * k, 8)], v.at[pl.ds(3 * h, 3), :, g], z2s.at[k], z2r.at[r], row=k
        )

    def second_from(k):
        return remote(
            w1.at[:, pl.ds(8 * r, 8)], v.at[pl.ds(3 * (k % 2), 3), :, k // 2], z2s.at[k], z2r.at[k], row=k
        )

    def widen_rows(k):
        for j in range(8):
            p = 8 * k + j
            w1[:, p] = z1[:, maps_ref[s, p]]

    def send_second(j):
        k = lax.rem(r + j, ROWS)
        widen_rows(k)
        second(k).start()

    each(1, 16, send_second)
    widen_rows(r)
    own2 = pltpu.make_async_copy(w1.at[:, pl.ds(8 * r, 8)], v.at[pl.ds(3 * h, 3), :, g], lsem.at[2])
    own2.start()

    def corner_c(k):
        return remote(crn.at[s, :, :, r], crn.at[s, :, :, r], ccs.at[k], ccr.at[r], row=k)

    def corner_c_from(k):
        return remote(crn.at[s, :, :, k], crn.at[s, :, :, k], ccs.at[k], ccr.at[k], row=k)

    @pl.when(holds)
    def _():
        @pl.when(c > 0)
        def _():
            corner_b(c).wait_recv()
        each(1, 16, lambda j: corner_c(lax.rem(r + j, ROWS)).start())

    own2.wait()
    each(1, 16, lambda j: second_from(lax.rem(r + j, ROWS)).wait_recv())

    def third(k):
        return remote(
            v.at[:, k // 2, pl.ds(4 * (k % 2), 4)], z3.at[pl.ds(6 * c, 6)], z3s.at[k], z3r.at[c], col=k
        )

    def third_from(k):
        return remote(
            v.at[:, c // 2, pl.ds(4 * (c % 2), 4)], z3.at[pl.ds(6 * k, 6)], z3s.at[k], z3r.at[k], col=k
        )
    each(1, 16, lambda j: third(lax.rem(c + j, COLS)).start())
    own3 = pltpu.make_async_copy(
        v.at[:, c // 2, pl.ds(4 * (c % 2), 4)], z3.at[pl.ds(6 * c, 6)], lsem.at[3]
    )
    own3.start()

    def corner_rest(k):
        @pl.when(k != r)
        def _():
            corner_c_from(k).wait_recv()

    each(0, 8, corner_rest)
    swap = remote(crn.at[s], crn.at[s], sws.at[0], swr.at[0], sib=other)
    swap_back = remote(crn.at[s], crn.at[other], sws.at[0], swr.at[0], sib=other)
    swap.start()
    swap_back.wait_recv()
    for p in range(3):
        for q in range(3):
            total = pivot_ref[128 * p:128 * (p + 1), 128 * q:128 * (q + 1)].astype(F32)
            for child in range(2):
                i, j = maps_ref[child, p], maps_ref[child, q]
                present = (i < 3) & (j < 3)
                block = crn[child, jnp.minimum(j, 2), jnp.minimum(i, 2)].astype(F32).reshape(128, 128)
                total = total + jnp.where(present, block, 0.0)
            a_ref[128 * p:128 * (p + 1), 128 * q:128 * (q + 1)] = total
    factor_inverse(a_ref, parent_inv, s_ref, i_ref, l_ref)

    own3.wait()
    each(1, 16, lambda j: third_from(lax.rem(c + j, COLS)).wait_recv())

    def strip(p):
        return z3[maps_ref[s, p]]

    for p in range(3):
        fs[p] = strip(p)
    swap_pivots = remote(fs, fr, sws.at[1], swr.at[1], sib=other)
    swap_pivots.start()

    def half(k):
        return remote(xs.at[pl.ds(4 * k, 4)], xr.at[pl.ds(4 * k, 4)], xss.at[k], xsr.at[k], sib=other)

    def send_half(j):
        k = lax.rem(c + j, COLS)
        for q in range(4):
            xs[4 * k + q] = strip(64 * other + 4 * k + q)
        half(k).start()

    each(1, 17, send_half)

    swap_pivots.wait_recv()
    first_rows = (r == 0) & (c < 6)
    start_row = pl.multiple_of(64 * jnp.minimum(c, 5), 64)
    anchor = jnp.where(first_rows, pivot_ref[pl.ds(start_row, 64), :].astype(F32), 0.0)
    rows = jnp.concatenate(
        [fs[p].astype(F32).reshape(64, 128) + fr[p].astype(F32).reshape(64, 128) for p in range(3)], axis=1
    )
    piece = mm_nt(rows + anchor, parent_inv[...]).astype(BF16)
    prow[c] = piece

    mine = pl.ds(pl.multiple_of(32 * s, 32), 32)
    theirs = pl.ds(pl.multiple_of(32 * other, 32), 32)

    def gather_rows(k):
        return remote(prow.at[c, mine], prow.at[c, mine], g1s.at[k], g1r.at[c], col=k)

    def gather_rows_from(k):
        return remote(prow.at[c, mine], prow.at[k, mine], g1s.at[k], g1r.at[k], col=k)

    def hand_rows(k):
        return remote(prow.at[k, mine], prow.at[k, mine], hs.at[k], hr.at[k], sib=other)

    def hand_rows_from(k):
        return remote(prow.at[k, mine], prow.at[k, theirs], hs.at[k], hr.at[k], sib=other)

    def gather_cols(k):
        return remote(prow.at[c], pcol.at[c % 8], g2s.at[k], g2r.at[c % 8], row=k, col=cols_to)

    def gather_cols_from(k):
        return remote(
            prow.at[c], pcol.at[k], g2s.at[k], g2r.at[k], row=cols_from_row, col=cols_from_col + k
        )

    def is_other(k):
        return jnp.logical_not((k == r) & (cols_to == c))

    @pl.when(sends_cols)
    def _():
        def go(j):
            k = lax.rem(r + j, ROWS)

            @pl.when(is_other(k))
            def _():
                gather_cols(k).start()

            @pl.when(jnp.logical_not(is_other(k)))
            def _():
                pcol[c % 8] = piece

        each(1, 17, go)

    each(1, 16, lambda j: gather_rows(lax.rem(c + j, COLS)).start())

    def fourth(k):
        return remote(y.at[pl.ds(4 * k, 4)], z4.at[c], z4s.at[k], z4r.at[c], col=k)

    def fourth_from(k):
        return remote(y.at[pl.ds(4 * k, 4)], z4.at[k], z4s.at[k], z4r.at[k], col=k)

    def both(k, q):
        return (strip(64 * s + 4 * k + q).astype(F32) + xr[4 * k + q].astype(F32)).astype(BF16)

    def send_fourth(j):
        k = lax.rem(c + j, COLS)
        half(k).wait_recv()
        for q in range(4):
            y[4 * k + q] = both(k, q)
        fourth(k).start()

    each(1, 16, send_fourth)
    half(c).wait_recv()
    for q in range(4):
        z4[c, q] = both(c, q)

    def cols_rest(k):
        @pl.when(jnp.logical_not((cols_from_row == r) & (cols_from_col + k == c)))
        def _():
            gather_cols_from(k).wait_recv()

    each(0, 8, cols_rest)

    def hand(j):
        k = lax.rem(c + COLS - j, COLS)
        gather_rows_from(k).wait_recv()
        hand_rows(k).start()

    each(1, 16, hand)
    for chunk in range(4):
        def rows_rest(k):
            @pl.when(k != c)
            def _():
                hand_rows_from(k).wait_recv()
                fourth_from(k).wait_recv()

        each(4 * chunk, 4 * chunk + 4, rows_rest)
        left = prow[4 * chunk:4 * chunk + 4].reshape(256, 384)
        panel_ref[256 * chunk:256 * (chunk + 1), :] = left
        row_ids = 1024 * r + 256 * chunk + lax.broadcasted_iota(jnp.int32, (256, 128), 0)
        for q in range(4):
            right = pcol[2 * q:2 * q + 2].reshape(128, 384)
            front = z4[4 * chunk:4 * chunk + 4, q].astype(F32).reshape(256, 128)
            value = front - dot_nt(left, right)
            col_ids = 512 * (16 * s + c) + 128 * q + lax.broadcasted_iota(jnp.int32, (256, 128), 1)
            value = jnp.where((row_ids >= 384) & (col_ids >= 384), value, 0.0)
            update_ref[256 * chunk:256 * (chunk + 1), 128 * q:128 * (q + 1)] = value.astype(BF16)

    @pl.when(is_root)
    def _():
        each(1, 16, lambda j: scatter(lax.rem(r + j, ROWS)).wait_send())

    to_others(lambda k: spread(k).wait_send())

    @pl.when(at_root)
    def _():
        each(1, 8, lambda k: corner_a(k).wait_send())

    @pl.when(holds & (c == 0))
    def _():
        each(1, 16, lambda k: corner_b(k).wait_send())

    @pl.when(holds)
    def _():
        each(1, 16, lambda j: corner_c(lax.rem(r + j, ROWS)).wait_send())

    @pl.when(sends_cols)
    def _():
        def gone(k):
            @pl.when(is_other(k))
            def _():
                gather_cols(k).wait_send()

        each(0, 16, gone)

    def all_gone(j):
        k = lax.rem(r + j, ROWS)
        first(k).wait_send()
        second(k).wait_send()
        k = lax.rem(c + j, COLS)
        third(k).wait_send()
        fourth(k).wait_send()
        gather_rows(k).wait_send()
        hand_rows(k).wait_send()

    each(1, 16, all_gone)
    each(0, 16, lambda k: half(k).wait_send())
    swap.wait_send()
    swap_pivots.wait_send()


def front_step(maps, trailing, border, child, pivot):
    vmem = pl.BlockSpec(memory_space=pltpu.VMEM)
    dma = pltpu.SemaphoreType.DMA
    buffers = [
        (16, 48, 384),
        (768, 384), (768, 384),
        (6, 6, 8, 16, 128),
        (3, 97, 16, 128),
        (3, 128, 16, 128),
        (6, 8, 8, 16, 128),
        (97, 4, 16, 128),
        (64, 4, 16, 128), (64, 4, 16, 128),
        (3, 4, 16, 128), (3, 4, 16, 128),
        (64, 4, 16, 128),
        (16, 4, 4, 16, 128),
        (16, 64, 384), (8, 64, 384),
        (2, 3, 3, 8, 16, 128),
    ]
    counts = [16, 1] + [16] * 14 + [8, 1, 16, 1, 16, 8, 2, 2, 16, 16, 16, 16, 5]
    return pl.pallas_call(
        front_kernel,
        out_shape=(
            jax.ShapeDtypeStruct((1024, 384), BF16),
            jax.ShapeDtypeStruct((1024, 512), BF16),
        ),
        in_specs=[pl.BlockSpec(memory_space=pltpu.SMEM)] + [vmem] * 4,
        out_specs=(vmem, vmem),
        scratch_shapes=[pltpu.VMEM(shape, BF16) for shape in buffers]
        + [pltpu.VMEM((384, 384), F32)]
        + FACTOR_SCRATCH
        + [dma((count,)) for count in counts],
        compiler_params=pltpu.CompilerParams(
            collective_id=0, has_side_effects=True, vmem_limit_bytes=50 << 20
        ),
        cost_estimate=pl.CostEstimate(flops=10**10, bytes_accessed=10**8, transcendentals=0),
    )(maps, trailing, border, child, pivot)


def inverse_maps(child_maps):
    matches = child_maps[:, :, None] == jnp.arange(128, dtype=jnp.int32)
    source = jnp.arange(96, dtype=jnp.int32)[None, :, None]
    return jnp.min(jnp.where(matches, source, 96), axis=1).astype(jnp.int32)


def shards(child_pivot, child_border, child_trailing, parent_pivot, child_maps):
    border = child_border[0].reshape(16, 48, 384)
    return front_step(inverse_maps(child_maps), child_trailing[0], border, child_pivot[0], parent_pivot)


def solution(mesh):
    placed = (P("sib", None, None), P("sib", "row", None), P("sib", "row", "col"), P(), P())
    return jax.shard_map(
        shards,
        mesh=mesh,
        in_specs=placed,
        out_specs=(P("row", None), P("row", ("sib", "col"))),
        check_vma=False,
    )
```

```python
import jax
import jax.numpy as jnp
from jax import lax
from jax.experimental import pallas as pl
from jax.experimental.pallas import tpu as pltpu
from jax.sharding import PartitionSpec as P

BF16 = jnp.bfloat16
F32 = jnp.float32
HIGHEST = lax.Precision.HIGHEST
NT = (((1,), (1,)), ((), ()))
MESH = pl.DeviceIdType.MESH
ROWS = 16
COLS = 16


def mm(a, b):
    return jnp.dot(a, b, precision=HIGHEST, preferred_element_type=F32)


def mm_nt(a, b):
    return lax.dot_general(a, b, NT, precision=HIGHEST, preferred_element_type=F32)


def dot_nt(a, b):
    return lax.dot_general(a, b, NT, preferred_element_type=F32)


def block_inverse(s_ref, i_ref):
    n = 128
    rows = lax.broadcasted_iota(jnp.int32, (n, n), 0)
    cols = lax.broadcasted_iota(jnp.int32, (n, n), 1)
    x = s_ref[...]
    m = jnp.where(rows == cols, 1.0, 0.0)
    for panel in range(n // 8):
        for o in range(0, 8, 4):
            j = 8 * panel + o
            w = [jnp.broadcast_to(x[:, j + k:j + k + 1], x.shape) for k in range(4)]
            g = [[w[q][o + p:o + p + 1, :] for q in range(4)] for p in range(4)]
            xr = [x[o + k:o + k + 1, :] for k in range(4)]
            mr = [m[o + k:o + k + 1, :] for k in range(4)]
            a, b, c = g[0][0], g[1][0], g[1][1]
            inv = 1.0 / (a * c - b * b)
            ci, bi, ai = c * inv, b * inv, a * inv
            def pair(r1, r2, ci=ci, bi=bi, ai=ai):
                return ci * r1 - bi * r2, ai * r2 - bi * r1
            x1p, x2p = pair(xr[0], xr[1])
            m1p, m2p = pair(mr[0], mr[1])
            i_ref[j:j + 1, :] = mr[0] * lax.rsqrt(a)
            i_ref[j + 1:j + 2, :] = m2p * lax.rsqrt(ai)
            p20, p21 = pair(g[2][0], g[2][1])
            p30, p31 = pair(g[3][0], g[3][1])
            a2 = g[2][2] - (g[2][0] * p20 + g[2][1] * p21)
            b2 = g[3][2] - (g[3][0] * p20 + g[3][1] * p21)
            c2 = g[3][3] - (g[3][0] * p30 + g[3][1] * p31)
            inv2 = 1.0 / (a2 * c2 - b2 * b2)
            ci2, bi2, ai2 = c2 * inv2, b2 * inv2, a2 * inv2
            x3 = xr[2] - g[2][0] * x1p - g[2][1] * x2p
            x4 = xr[3] - g[3][0] * x1p - g[3][1] * x2p
            m3 = mr[2] - g[2][0] * m1p - g[2][1] * m2p
            m4 = mr[3] - g[3][0] * m1p - g[3][1] * m2p
            x3p, x4p = pair(x3, x4, ci2, bi2, ai2)
            m3p, m4p = pair(m3, m4, ci2, bi2, ai2)
            i_ref[j + 2:j + 3, :] = m3 * lax.rsqrt(a2)
            i_ref[j + 3:j + 4, :] = m4p * lax.rsqrt(ai2)
            if o == 4:
                x, m = x[8:, :], m[8:, :]
                w = [t[8:, :] for t in w]
                if panel == n // 8 - 1:
                    break
            f1, f2 = pair(w[0], w[1])
            u3 = w[2] - f1 * g[2][0] - f2 * g[2][1]
            u4 = w[3] - f1 * g[3][0] - f2 * g[3][1]
            x = x - w[0] * x1p - w[1] * x2p - u3 * x3p - u4 * x4p
            m = m - w[0] * m1p - w[1] * m2p - u3 * m3p - u4 * m4p


def factor_inverse(a_ref, out_ref, s_ref, i_ref, l_ref, between=None):
    n = 384
    a = a_ref[...]
    rows = lax.broadcasted_iota(jnp.int32, (n, n), 0)
    cols = lax.broadcasted_iota(jnp.int32, (n, n), 1)
    diag = jnp.where(rows == cols, a, 0.0)
    dr = lax.rsqrt(jnp.sum(diag, axis=0, keepdims=True))
    dc = lax.rsqrt(jnp.sum(diag, axis=1, keepdims=True))
    a_ref[...] = a * dr * dc
    b = [pl.ds(128 * k, 128) for k in range(3)]
    out_ref[...] = jnp.zeros((n, n), F32)
    s_ref[...] = a_ref[b[0], b[0]]

    def body(k, carry):
        block_inverse(s_ref, i_ref)
        inv = i_ref[...]

        @pl.when(k == 0)
        def _():
            out_ref[b[0], b[0]] = inv
            l21 = mm_nt(a_ref[b[1], b[0]], inv)
            s_ref[...] = a_ref[b[1], b[1]] - mm_nt(l21, l21)
            l31 = mm_nt(a_ref[b[2], b[0]], inv)
            a_ref[b[2], b[1]] = a_ref[b[2], b[1]] - mm_nt(l31, l21)
            a_ref[b[2], b[2]] = a_ref[b[2], b[2]] - mm_nt(l31, l31)
            l_ref[0] = mm(l21, inv)
            l_ref[1] = mm(l31, inv)
            if between is not None:
                between()

        @pl.when(k == 1)
        def _():
            out_ref[b[1], b[1]] = inv
            l32 = mm_nt(a_ref[b[2], b[1]], inv)
            s_ref[...] = a_ref[b[2], b[2]] - mm_nt(l32, l32)
            x21 = -mm(inv, l_ref[0])
            out_ref[b[1], b[0]] = x21
            l_ref[1] = l_ref[1] + mm(l32, x21)
            l_ref[2] = mm(l32, inv)

        @pl.when(k == 2)
        def _():
            out_ref[b[2], b[2]] = inv
            out_ref[b[2], b[0]] = -mm(inv, l_ref[1])
            out_ref[b[2], b[1]] = -mm(inv, l_ref[2])

        return carry

    lax.fori_loop(0, 3, body, 0)
    out_ref[...] = out_ref[...] * dr


FACTOR_SCRATCH = [
    pltpu.VMEM((384, 384), F32),
    pltpu.VMEM((128, 128), F32),
    pltpu.VMEM((128, 128), F32),
    pltpu.VMEM((3, 128, 128), F32),
]


def panel_of(border, inverse):
    high = inverse.astype(BF16)
    rest = inverse - high.astype(F32)
    middle = rest.astype(BF16)
    low = (rest - middle.astype(F32)).astype(BF16)
    return (dot_nt(border, high) + (dot_nt(border, middle) + dot_nt(border, low))).astype(BF16)


def front_kernel(
    maps_ref, trailing_ref, border_ref, child_ref, pivot_ref,
    panel_ref, update_ref,
    bx, pr, pc, u, z1, w1, z3, zf, xs, xr, fs, fr, y, z4, prow, pcol, crn, parent_inv,
    a_ref, s_ref, i_ref, l_ref,
    b1s, b1r, b2s, b2r, z1s, z1r, z2s, z2r, z4s, z4r, g1s, g1r, g2s, g2r,
    cas, car, cbs, cbr, ccs, ccr, sws, swr, xss, xsr, hs, hr, lsem, told,
):
    s = lax.axis_index("sib")
    r = lax.axis_index("row")
    c = lax.axis_index("col")
    other = 1 - s
    g, h = r // 2, r % 2

    sends_cols = s == r // 8
    cols_to = 2 * (r % 8) + c // 8
    cols_from_row = 8 * s + c // 2
    cols_from_col = 8 * (c % 2)

    def remote(src, dst, send, recv, **to):
        return pltpu.make_async_remote_copy(
            src_ref=src, dst_ref=dst, send_sem=send, recv_sem=recv, device_id=to, device_id_type=MESH
        )

    def each(first, last, body):
        def step(k, carry):
            body(k)
            return carry
        lax.fori_loop(first, last, step, 0)

    barrier = pltpu.get_barrier_semaphore()

    def greet(j):
        pl.semaphore_signal(barrier, inc=1, device_id={"row": lax.rem(r + j, ROWS)}, device_id_type=MESH)
        pl.semaphore_signal(barrier, inc=1, device_id={"col": lax.rem(c + j, COLS)}, device_id_type=MESH)

    each(1, 16, greet)
    pl.semaphore_signal(barrier, inc=1, device_id={"sib": other}, device_id_type=MESH)

    pl.semaphore_wait(barrier, 31)

    def greet_again(j):
        pl.semaphore_signal(told, inc=1, device_id={"col": lax.rem(c + j, COLS)}, device_id_type=MESH)

    each(1, 16, greet_again)
    keeps = c % 2 == r // 8

    is_root = r == c

    def scatter(k):
        return remote(border_ref.at[k], bx.at[k], b1s.at[k], b1r.at[0], row=k)

    def scatter_here():
        return remote(border_ref.at[r], bx.at[r], b1s.at[r], b1r.at[0], row=c)

    def spread(k):
        return remote(bx.at[r], bx.at[r], b2s.at[k], b2r.at[r], row=k)

    def spread_from(k):
        return remote(bx.at[r], bx.at[k], b2s.at[k], b2r.at[k], row=k)

    def to_others(body):
        def go(j):
            k = lax.rem(r + j, ROWS)

            @pl.when(k != c)
            def _():
                body(k)

        each(1, 16, go)

    own_border = pltpu.make_async_copy(border_ref, bx, lsem.at[4])

    @pl.when(is_root)
    def _():
        each(1, 16, lambda j: scatter(lax.rem(r + j, ROWS)).start())
        own_border.start()
        own_border.wait()

    def spread_border():
        @pl.when(jnp.logical_not(is_root))
        def _():
            scatter_here().wait_recv()

        to_others(lambda k: spread(k).start())

    a_ref[...] = child_ref[...].astype(F32)
    factor_inverse(a_ref, parent_inv, s_ref, i_ref, l_ref, spread_border)
    inverse = parent_inv[...]
    pr[...] = panel_of(border_ref[...].reshape(768, 384), inverse)

    @pl.when(jnp.logical_not(is_root))
    def _():
        each(1, 16, lambda j: spread_from(lax.rem(r + j, ROWS)).wait_recv())

    pc[...] = panel_of(bx[...].reshape(768, 384), inverse)
    for i in range(6):
        rows = pl.ds(128 * i, 128)
        value = trailing_ref[rows, :].astype(F32) - dot_nt(pr[rows, :], pc[...])
        value = value.astype(BF16)
        for q in range(6):
            u[q, i] = value[:, 128 * q:128 * (q + 1)].reshape(8, 16, 128)

    at_root = (r == 0) & (c == 0)
    holds = r < 8

    def corner_a(k):
        return remote(u.at[0:3, 0:3, k], crn.at[s, :, :, k], cas.at[k], car.at[0], row=k)

    @pl.when(at_root)
    def _():
        each(1, 8, lambda k: corner_a(k).start())
        own = pltpu.make_async_copy(u.at[0:3, 0:3, 0], crn.at[s, :, :, 0], lsem.at[0])
        own.start()
        own.wait()

    def corner_b(k):
        return remote(crn.at[s, :, :, r], crn.at[s, :, :, r], cbs.at[k], cbr.at[0], col=k)

    def corner_c(k):
        return remote(crn.at[s, :, :, r], crn.at[s, :, :, r], ccs.at[k], ccr.at[r], row=k)

    def corner_c_from(k):
        return remote(crn.at[s, :, :, k], crn.at[s, :, :, k], ccs.at[k], ccr.at[k], row=k)

    def first(k):
        return remote(
            u.at[pl.ds(3 * (k % 2), 3), :, k // 2], z1.at[:, pl.ds(6 * r, 6)], z1s.at[k], z1r.at[r], row=k
        )

    def first_from(k):
        return remote(
            u.at[pl.ds(3 * h, 3), :, g], z1.at[:, pl.ds(6 * k, 6)], z1s.at[k], z1r.at[k], row=k
        )

    each(1, 4, lambda j: first(lax.rem(r + j, ROWS)).start())
    own1 = pltpu.make_async_copy(u.at[pl.ds(3 * h, 3), :, g], z1.at[:, pl.ds(6 * r, 6)], lsem.at[1])
    own1.start()

    @pl.when(holds & (c == 0))
    def _():
        @pl.when(r > 0)
        def _():
            corner_a(r).wait_recv()
        each(1, 16, lambda k: corner_b(k).start())

    each(4, 9, lambda j: first(lax.rem(r + j, ROWS)).start())
    z1[:, 96] = jnp.zeros((3, 16, 128), BF16)
    z3[96] = jnp.zeros((4, 16, 128), BF16)
    zf[3] = jnp.zeros((4, 16, 128), BF16)

    @pl.when(holds)
    def _():
        @pl.when(c > 0)
        def _():
            corner_b(c).wait_recv()
        each(1, 16, lambda j: corner_c(lax.rem(r + j, ROWS)).start())

    each(9, 16, lambda j: first(lax.rem(r + j, ROWS)).start())

    def corner_rest(k):
        @pl.when(k != r)
        def _():
            corner_c_from(k).wait_recv()

    each(0, 8, corner_rest)
    swap = remote(crn.at[s], crn.at[s], sws.at[0], swr.at[0], sib=other)
    swap_back = remote(crn.at[s], crn.at[other], sws.at[0], swr.at[0], sib=other)
    swap.start()
    own1.wait()
    each(1, 16, lambda j: first_from(lax.rem(r + j, ROWS)).wait_recv())
    pl.semaphore_wait(told, 15)

    def second(k, l):
        return remote(
            w1.at[:, 8 * k + l // 2], z3.at[pl.ds(6 * c + 3 * h, 3), g % 4],
            z2s.at[8 * k + l // 2], z2r.at[8 * c + r % 8], row=k, col=l
        )

    def second_from(k, l):
        return remote(
            w1.at[:, 8 * r + c // 2], z3.at[pl.ds(6 * l + 3 * (k % 2), 3), k // 2 % 4],
            z2s.at[8 * r + c // 2], z2r.at[8 * l + k % 8], row=k, col=l
        )

    def here2():
        return pltpu.make_async_copy(
            w1.at[:, 8 * r + c // 2], z3.at[pl.ds(6 * c + 3 * h, 3), g % 4], lsem.at[2]
        )

    def send_second(j):
        k = lax.rem(r + j, ROWS)

        def go(i):
            l = lax.rem(2 * i + c, COLS) // 2 * 2 + r // 8
            p = 8 * k + l // 2
            w1[:, p] = z1[:, maps_ref[s, p]]

            @pl.when((k == r) & (l == c))
            def _():
                here2().start()

            @pl.when(jnp.logical_not((k == r) & (l == c)))
            def _():
                second(k, l).start()

        each(0, 8, go)

    each(1, 17, send_second)

    swap_back.wait_recv()
    for p in range(3):
        for q in range(3):
            total = pivot_ref[128 * p:128 * (p + 1), 128 * q:128 * (q + 1)].astype(F32)
            for child in range(2):
                i, j = maps_ref[child, p], maps_ref[child, q]
                present = (i < 3) & (j < 3)
                block = crn[child, jnp.minimum(j, 2), jnp.minimum(i, 2)].astype(F32).reshape(128, 128)
                total = total + jnp.where(present, block, 0.0)
            a_ref[128 * p:128 * (p + 1), 128 * q:128 * (q + 1)] = total
    factor_inverse(a_ref, parent_inv, s_ref, i_ref, l_ref)

    @pl.when(keeps)
    def _():
        here2().wait()

    def not_self(k, l):
        return jnp.logical_not((k == r) & (l == c))

    def pivots_rest(j):
        k = 8 * (c % 2) + 2 * j

        @pl.when(not_self(k, 0))
        def _():
            second_from(k, 0).wait_recv()

    each(0, 4, pivots_rest)
    for p in range(3):
        zf[p] = z3[p]
    for p in range(3):
        fs[p] = zf[jnp.minimum(maps_ref[s, p], 3)]
    swap_pivots = remote(fs, fr, sws.at[1], swr.at[1], sib=other)
    swap_pivots.start()
    swap_pivots.wait_recv()
    first_rows = (r == 0) & (c < 6)
    start_row = pl.multiple_of(64 * jnp.minimum(c, 5), 64)
    anchor = jnp.where(first_rows, pivot_ref[pl.ds(start_row, 64), :].astype(F32), 0.0)
    rows = jnp.concatenate(
        [fs[p].astype(F32).reshape(64, 128) + fr[p].astype(F32).reshape(64, 128) for p in range(3)], axis=1
    )
    piece = mm_nt(rows + anchor, parent_inv[...]).astype(BF16)
    prow[c] = piece

    mine = pl.ds(pl.multiple_of(32 * s, 32), 32)
    theirs = pl.ds(pl.multiple_of(32 * other, 32), 32)

    def gather_rows(k):
        return remote(prow.at[c, mine], prow.at[c, mine], g1s.at[k], g1r.at[c], col=k)

    def gather_rows_from(k):
        return remote(prow.at[c, mine], prow.at[k, mine], g1s.at[k], g1r.at[k], col=k)

    def hand_rows(k):
        return remote(prow.at[k, mine], prow.at[k, mine], hs.at[k], hr.at[k], sib=other)

    def hand_rows_from(k):
        return remote(prow.at[k, mine], prow.at[k, theirs], hs.at[k], hr.at[k], sib=other)

    def gather_cols(k):
        return remote(prow.at[c], pcol.at[c % 8], g2s.at[k], g2r.at[c % 8], row=k, col=cols_to)

    def gather_cols_from(k):
        return remote(
            prow.at[c], pcol.at[k], g2s.at[k], g2r.at[k], row=cols_from_row, col=cols_from_col + k
        )

    def is_other(k):
        return jnp.logical_not((k == r) & (cols_to == c))

    @pl.when(sends_cols)
    def _():
        def go(j):
            k = lax.rem(r + j, ROWS)

            @pl.when(is_other(k))
            def _():
                gather_cols(k).start()

            @pl.when(jnp.logical_not(is_other(k)))
            def _():
                pcol[c % 8] = piece

        each(1, 17, go)

    each(1, 16, lambda j: gather_rows(lax.rem(c + j, COLS)).start())

    def second_rest(j):
        k, l = 8 * (c % 2) + j % 8, j // 8

        @pl.when(not_self(k, l) & ((l > 0) | (k % 2 == 1)))
        def _():
            second_from(k, l).wait_recv()

    each(0, 128, second_rest)

    def strip(p):
        return z3[maps_ref[s, p]]

    def half(k):
        return remote(xs.at[pl.ds(4 * k, 4)], xr.at[pl.ds(4 * k, 4)], xss.at[k], xsr.at[k], sib=other)

    def send_half(j):
        k = lax.rem(c + j, COLS)
        for q in range(4):
            xs[4 * k + q] = strip(64 * other + 4 * k + q)
        half(k).start()

    each(1, 17, send_half)

    def fourth(k):
        return remote(y.at[pl.ds(4 * k, 4)], z4.at[c], z4s.at[k], z4r.at[c], col=k)

    def fourth_from(k):
        return remote(y.at[pl.ds(4 * k, 4)], z4.at[k], z4s.at[k], z4r.at[k], col=k)

    def both(k, q):
        return (strip(64 * s + 4 * k + q).astype(F32) + xr[4 * k + q].astype(F32)).astype(BF16)

    def send_fourth(j):
        k = lax.rem(c + j, COLS)
        half(k).wait_recv()
        for q in range(4):
            y[4 * k + q] = both(k, q)
        fourth(k).start()

    each(1, 16, send_fourth)
    half(c).wait_recv()
    for q in range(4):
        z4[c, q] = both(c, q)

    def cols_rest(k):
        @pl.when(jnp.logical_not((cols_from_row == r) & (cols_from_col + k == c)))
        def _():
            gather_cols_from(k).wait_recv()

    each(0, 8, cols_rest)

    def hand(j):
        k = lax.rem(c + COLS - j, COLS)
        gather_rows_from(k).wait_recv()
        hand_rows(k).start()

    each(1, 16, hand)
    for chunk in range(4):
        def rows_rest(k):
            @pl.when(k != c)
            def _():
                hand_rows_from(k).wait_recv()
                fourth_from(k).wait_recv()

        each(4 * chunk, 4 * chunk + 4, rows_rest)
        left = prow[4 * chunk:4 * chunk + 4].reshape(256, 384)
        panel_ref[256 * chunk:256 * (chunk + 1), :] = left
        row_ids = 1024 * r + 256 * chunk + lax.broadcasted_iota(jnp.int32, (256, 128), 0)
        for q in range(4):
            right = pcol[2 * q:2 * q + 2].reshape(128, 384)
            front = z4[4 * chunk:4 * chunk + 4, q].astype(F32).reshape(256, 128)
            value = front - dot_nt(left, right)
            col_ids = 512 * (16 * s + c) + 128 * q + lax.broadcasted_iota(jnp.int32, (256, 128), 1)
            value = jnp.where((row_ids >= 384) & (col_ids >= 384), value, 0.0)
            update_ref[256 * chunk:256 * (chunk + 1), 128 * q:128 * (q + 1)] = value.astype(BF16)

    @pl.when(is_root)
    def _():
        each(1, 16, lambda j: scatter(lax.rem(r + j, ROWS)).wait_send())

    to_others(lambda k: spread(k).wait_send())

    @pl.when(at_root)
    def _():
        each(1, 8, lambda k: corner_a(k).wait_send())

    @pl.when(holds & (c == 0))
    def _():
        each(1, 16, lambda k: corner_b(k).wait_send())

    @pl.when(holds)
    def _():
        each(1, 16, lambda j: corner_c(lax.rem(r + j, ROWS)).wait_send())

    @pl.when(sends_cols)
    def _():
        def gone(k):
            @pl.when(is_other(k))
            def _():
                gather_cols(k).wait_send()

        each(0, 16, gone)

    def all_gone(j):
        k = lax.rem(r + j, ROWS)
        first(k).wait_send()
        k = lax.rem(c + j, COLS)
        fourth(k).wait_send()
        gather_rows(k).wait_send()
        hand_rows(k).wait_send()

    each(1, 16, all_gone)

    def second_gone(j):
        k, l = j // 8, 2 * (j % 8) + r // 8

        @pl.when(jnp.logical_not((k == r) & (l == c)))
        def _():
            second(k, l).wait_send()

    each(0, 128, second_gone)
    each(0, 16, lambda k: half(k).wait_send())
    swap.wait_send()
    swap_pivots.wait_send()


def front_step(maps, trailing, border, child, pivot):
    vmem = pl.BlockSpec(memory_space=pltpu.VMEM)
    dma = pltpu.SemaphoreType.DMA
    buffers = [
        (16, 48, 384),
        (768, 384), (768, 384),
        (6, 6, 8, 16, 128),
        (3, 97, 16, 128),
        (3, 128, 16, 128),
        (97, 4, 16, 128),
        (4, 4, 16, 128),
        (64, 4, 16, 128), (64, 4, 16, 128),
        (3, 4, 16, 128), (3, 4, 16, 128),
        (64, 4, 16, 128),
        (16, 4, 4, 16, 128),
        (16, 64, 384), (8, 64, 384),
        (2, 3, 3, 8, 16, 128),
    ]
    counts = [16, 1] + [16] * 4 + [128] * 2 + [16] * 6 + [8, 1, 16, 1, 16, 8, 2, 2, 16, 16, 16, 16, 5]
    return pl.pallas_call(
        front_kernel,
        out_shape=(
            jax.ShapeDtypeStruct((1024, 384), BF16),
            jax.ShapeDtypeStruct((1024, 512), BF16),
        ),
        in_specs=[pl.BlockSpec(memory_space=pltpu.SMEM)] + [vmem] * 4,
        out_specs=(vmem, vmem),
        scratch_shapes=[pltpu.VMEM(shape, BF16) for shape in buffers]
        + [pltpu.VMEM((384, 384), F32)]
        + FACTOR_SCRATCH
        + [dma((count,)) for count in counts]
        + [pltpu.SemaphoreType.REGULAR],
        compiler_params=pltpu.CompilerParams(
            collective_id=0, has_side_effects=True, vmem_limit_bytes=50 << 20
        ),
        cost_estimate=pl.CostEstimate(flops=10**10, bytes_accessed=10**8, transcendentals=0),
    )(maps, trailing, border, child, pivot)


def inverse_maps(child_maps):
    matches = child_maps[:, :, None] == jnp.arange(128, dtype=jnp.int32)
    source = jnp.arange(96, dtype=jnp.int32)[None, :, None]
    return jnp.min(jnp.where(matches, source, 96), axis=1).astype(jnp.int32)


def shards(child_pivot, child_border, child_trailing, parent_pivot, child_maps):
    border = child_border[0].reshape(16, 48, 384)
    return front_step(inverse_maps(child_maps), child_trailing[0], border, child_pivot[0], parent_pivot)


def solution(mesh):
    placed = (P("sib", None, None), P("sib", "row", None), P("sib", "row", "col"), P(), P())
    return jax.shard_map(
        shards,
        mesh=mesh,
        in_specs=placed,
        out_specs=(P("row", None), P("row", ("sib", "col"))),
        check_vma=False,
    )
```

```python
import jax
import jax.numpy as jnp
from jax import lax
from jax.experimental import pallas as pl
from jax.experimental.pallas import tpu as pltpu
from jax.sharding import PartitionSpec as P

BF16 = jnp.bfloat16
F32 = jnp.float32
HIGHEST = lax.Precision.HIGHEST
NT = (((1,), (1,)), ((), ()))
MESH = pl.DeviceIdType.MESH
ROWS = 16
COLS = 16


def mm(a, b):
    return jnp.dot(a, b, precision=HIGHEST, preferred_element_type=F32)


def mm_nt(a, b):
    return lax.dot_general(a, b, NT, precision=HIGHEST, preferred_element_type=F32)


def dot_nt(a, b):
    return lax.dot_general(a, b, NT, preferred_element_type=F32)


def block_inverse(s_ref, i_ref):
    n = 128
    rows = lax.broadcasted_iota(jnp.int32, (n, n), 0)
    cols = lax.broadcasted_iota(jnp.int32, (n, n), 1)
    x = s_ref[...]
    m = jnp.where(rows == cols, 1.0, 0.0)
    for panel in range(n // 8):
        for o in range(0, 8, 4):
            j = 8 * panel + o
            w = [jnp.broadcast_to(x[:, j + k:j + k + 1], x.shape) for k in range(4)]
            g = [[w[q][o + p:o + p + 1, :] for q in range(4)] for p in range(4)]
            xr = [x[o + k:o + k + 1, :] for k in range(4)]
            mr = [m[o + k:o + k + 1, :] for k in range(4)]
            a, b, c = g[0][0], g[1][0], g[1][1]
            inv = 1.0 / (a * c - b * b)
            ci, bi, ai = c * inv, b * inv, a * inv
            def pair(r1, r2, ci=ci, bi=bi, ai=ai):
                return ci * r1 - bi * r2, ai * r2 - bi * r1
            x1p, x2p = pair(xr[0], xr[1])
            m1p, m2p = pair(mr[0], mr[1])
            i_ref[j:j + 1, :] = mr[0] * lax.rsqrt(a)
            i_ref[j + 1:j + 2, :] = m2p * lax.rsqrt(ai)
            p20, p21 = pair(g[2][0], g[2][1])
            p30, p31 = pair(g[3][0], g[3][1])
            a2 = g[2][2] - (g[2][0] * p20 + g[2][1] * p21)
            b2 = g[3][2] - (g[3][0] * p20 + g[3][1] * p21)
            c2 = g[3][3] - (g[3][0] * p30 + g[3][1] * p31)
            inv2 = 1.0 / (a2 * c2 - b2 * b2)
            ci2, bi2, ai2 = c2 * inv2, b2 * inv2, a2 * inv2
            x3 = xr[2] - g[2][0] * x1p - g[2][1] * x2p
            x4 = xr[3] - g[3][0] * x1p - g[3][1] * x2p
            m3 = mr[2] - g[2][0] * m1p - g[2][1] * m2p
            m4 = mr[3] - g[3][0] * m1p - g[3][1] * m2p
            x3p, x4p = pair(x3, x4, ci2, bi2, ai2)
            m3p, m4p = pair(m3, m4, ci2, bi2, ai2)
            i_ref[j + 2:j + 3, :] = m3 * lax.rsqrt(a2)
            i_ref[j + 3:j + 4, :] = m4p * lax.rsqrt(ai2)
            if o == 4:
                x, m = x[8:, :], m[8:, :]
                w = [t[8:, :] for t in w]
                if panel == n // 8 - 1:
                    break
            f1, f2 = pair(w[0], w[1])
            u3 = w[2] - f1 * g[2][0] - f2 * g[2][1]
            u4 = w[3] - f1 * g[3][0] - f2 * g[3][1]
            x = x - w[0] * x1p - w[1] * x2p - u3 * x3p - u4 * x4p
            m = m - w[0] * m1p - w[1] * m2p - u3 * m3p - u4 * m4p


def factor_inverse(a_ref, out_ref, s_ref, i_ref, l_ref, between=None):
    n = 384
    a = a_ref[...]
    rows = lax.broadcasted_iota(jnp.int32, (n, n), 0)
    cols = lax.broadcasted_iota(jnp.int32, (n, n), 1)
    diag = jnp.where(rows == cols, a, 0.0)
    dr = lax.rsqrt(jnp.sum(diag, axis=0, keepdims=True))
    dc = lax.rsqrt(jnp.sum(diag, axis=1, keepdims=True))
    a_ref[...] = a * dr * dc
    b = [pl.ds(128 * k, 128) for k in range(3)]
    out_ref[...] = jnp.zeros((n, n), F32)
    s_ref[...] = a_ref[b[0], b[0]]

    def body(k, carry):
        block_inverse(s_ref, i_ref)
        inv = i_ref[...]

        @pl.when(k == 0)
        def _():
            out_ref[b[0], b[0]] = inv
            l21 = mm_nt(a_ref[b[1], b[0]], inv)
            s_ref[...] = a_ref[b[1], b[1]] - mm_nt(l21, l21)
            l31 = mm_nt(a_ref[b[2], b[0]], inv)
            a_ref[b[2], b[1]] = a_ref[b[2], b[1]] - mm_nt(l31, l21)
            a_ref[b[2], b[2]] = a_ref[b[2], b[2]] - mm_nt(l31, l31)
            l_ref[0] = mm(l21, inv)
            l_ref[1] = mm(l31, inv)
            if between is not None:
                between()

        @pl.when(k == 1)
        def _():
            out_ref[b[1], b[1]] = inv
            l32 = mm_nt(a_ref[b[2], b[1]], inv)
            s_ref[...] = a_ref[b[2], b[2]] - mm_nt(l32, l32)
            x21 = -mm(inv, l_ref[0])
            out_ref[b[1], b[0]] = x21
            l_ref[1] = l_ref[1] + mm(l32, x21)
            l_ref[2] = mm(l32, inv)

        @pl.when(k == 2)
        def _():
            out_ref[b[2], b[2]] = inv
            out_ref[b[2], b[0]] = -mm(inv, l_ref[1])
            out_ref[b[2], b[1]] = -mm(inv, l_ref[2])

        return carry

    lax.fori_loop(0, 3, body, 0)
    out_ref[...] = out_ref[...] * dr


FACTOR_SCRATCH = [
    pltpu.VMEM((384, 384), F32),
    pltpu.VMEM((128, 128), F32),
    pltpu.VMEM((128, 128), F32),
    pltpu.VMEM((3, 128, 128), F32),
]


def panel_of(border, inverse):
    high = inverse.astype(BF16)
    rest = inverse - high.astype(F32)
    middle = rest.astype(BF16)
    low = (rest - middle.astype(F32)).astype(BF16)
    return (dot_nt(border, high) + (dot_nt(border, middle) + dot_nt(border, low))).astype(BF16)


def front_kernel(
    maps_ref, trailing_ref, border_ref, child_ref, pivot_ref,
    panel_ref, update_ref,
    bx, pr, pc, u, cu, z1, w1, z3, zf, xs, xr, fs, fr, y, z4, prow, pcol, crn, parent_inv,
    a_ref, s_ref, i_ref, l_ref,
    b1s, b1r, b2s, b2r, z1s, z1r, z2s, z2r, z4s, z4r, g1s, g1r, g2s, g2r,
    cas, car, cbs, cbr, ccs, ccr, sws, swr, xss, xsr, hs, hr, lsem, told,
):
    s = lax.axis_index("sib")
    r = lax.axis_index("row")
    c = lax.axis_index("col")
    other = 1 - s
    g, h = r // 2, r % 2

    sends_cols = s == r // 8
    cols_to = 2 * (r % 8) + c // 8
    cols_from_row = 8 * s + c // 2
    cols_from_col = 8 * (c % 2)

    def remote(src, dst, send, recv, **to):
        return pltpu.make_async_remote_copy(
            src_ref=src, dst_ref=dst, send_sem=send, recv_sem=recv, device_id=to, device_id_type=MESH
        )

    def each(first, last, body):
        def step(k, carry):
            body(k)
            return carry
        lax.fori_loop(first, last, step, 0)

    barrier = pltpu.get_barrier_semaphore()

    def greet(j):
        pl.semaphore_signal(barrier, inc=1, device_id={"row": lax.rem(r + j, ROWS)}, device_id_type=MESH)
        pl.semaphore_signal(barrier, inc=1, device_id={"col": lax.rem(c + j, COLS)}, device_id_type=MESH)

    each(1, 16, greet)
    pl.semaphore_signal(barrier, inc=1, device_id={"sib": other}, device_id_type=MESH)

    pl.semaphore_wait(barrier, 31)

    def greet_again(j):
        pl.semaphore_signal(told, inc=1, device_id={"col": lax.rem(c + j, COLS)}, device_id_type=MESH)

    each(1, 16, greet_again)
    keeps = c % 2 == r // 8

    is_root = r == c

    def scatter(k):
        return remote(border_ref.at[k], bx.at[k], b1s.at[k], b1r.at[0], row=k)

    def scatter_here():
        return remote(border_ref.at[r], bx.at[r], b1s.at[r], b1r.at[0], row=c)

    def spread(k):
        return remote(bx.at[r], bx.at[r], b2s.at[k], b2r.at[r], row=k)

    def spread_from(k):
        return remote(bx.at[r], bx.at[k], b2s.at[k], b2r.at[k], row=k)

    def to_others(body):
        def go(j):
            k = lax.rem(r + j, ROWS)

            @pl.when(k != c)
            def _():
                body(k)

        each(1, 16, go)

    own_border = pltpu.make_async_copy(border_ref, bx, lsem.at[4])

    @pl.when(is_root)
    def _():
        each(1, 16, lambda j: scatter(lax.rem(r + j, ROWS)).start())
        own_border.start()
        own_border.wait()

    def spread_border():
        @pl.when(jnp.logical_not(is_root))
        def _():
            scatter_here().wait_recv()

        to_others(lambda k: spread(k).start())

    a_ref[...] = child_ref[...].astype(F32)
    factor_inverse(a_ref, parent_inv, s_ref, i_ref, l_ref, spread_border)
    inverse = parent_inv[...]
    pr[...] = panel_of(border_ref[...].reshape(768, 384), inverse)

    @pl.when(jnp.logical_not(is_root))
    def _():
        each(1, 16, lambda j: spread_from(lax.rem(r + j, ROWS)).wait_recv())

    pc[...] = panel_of(bx[...].reshape(768, 384), inverse)
    for i in range(6):
        rows = pl.ds(128 * i, 128)
        value = trailing_ref[rows, :].astype(F32) - dot_nt(pr[rows, :], pc[...])
        value = value.astype(BF16)
        for q in range(6):
            tile = value[:, 128 * q:128 * (q + 1)].reshape(8, 16, 128)
            u[q, i] = tile
            if q <= i < 3:
                cu[:, i * (i + 1) // 2 + q] = tile

    at_root = (r == 0) & (c == 0)
    holds = r < 8

    def corner_a(k):
        return remote(cu.at[k], crn.at[s, k], cas.at[k], car.at[0], row=k)

    @pl.when(at_root)
    def _():
        each(1, 8, lambda k: corner_a(k).start())
        own = pltpu.make_async_copy(cu.at[0], crn.at[s, 0], lsem.at[0])
        own.start()
        own.wait()

    def corner_b(k):
        return remote(crn.at[s, r], crn.at[s, r], cbs.at[k], cbr.at[0], col=k)

    def corner_c(k):
        return remote(crn.at[s, r], crn.at[s, r], ccs.at[k], ccr.at[r], row=k)

    def corner_c_from(k):
        return remote(crn.at[s, k], crn.at[s, k], ccs.at[k], ccr.at[k], row=k)

    def first(k):
        return remote(
            u.at[pl.ds(3 * (k % 2), 3), :, k // 2], z1.at[:, pl.ds(6 * r, 6)], z1s.at[k], z1r.at[r], row=k
        )

    def first_from(k):
        return remote(
            u.at[pl.ds(3 * h, 3), :, g], z1.at[:, pl.ds(6 * k, 6)], z1s.at[k], z1r.at[k], row=k
        )

    each(1, 4, lambda j: first(lax.rem(r + j, ROWS)).start())
    own1 = pltpu.make_async_copy(u.at[pl.ds(3 * h, 3), :, g], z1.at[:, pl.ds(6 * r, 6)], lsem.at[1])
    own1.start()

    @pl.when(holds & (c == 0))
    def _():
        @pl.when(r > 0)
        def _():
            corner_a(r).wait_recv()
        each(1, 16, lambda k: corner_b(k).start())

    each(4, 9, lambda j: first(lax.rem(r + j, ROWS)).start())
    z1[:, 96] = jnp.zeros((3, 16, 128), BF16)
    z3[96] = jnp.zeros((4, 16, 128), BF16)
    zf[3] = jnp.zeros((4, 16, 128), BF16)

    @pl.when(holds)
    def _():
        @pl.when(c > 0)
        def _():
            corner_b(c).wait_recv()
        each(1, 16, lambda j: corner_c(lax.rem(r + j, ROWS)).start())

    each(9, 16, lambda j: first(lax.rem(r + j, ROWS)).start())

    def corner_rest(k):
        @pl.when(k != r)
        def _():
            corner_c_from(k).wait_recv()

    each(0, 8, corner_rest)
    swap = remote(crn.at[s], crn.at[s], sws.at[0], swr.at[0], sib=other)
    swap_back = remote(crn.at[s], crn.at[other], sws.at[0], swr.at[0], sib=other)
    swap.start()
    own1.wait()
    each(1, 16, lambda j: first_from(lax.rem(r + j, ROWS)).wait_recv())
    pl.semaphore_wait(told, 15)

    def second(k, l):
        return remote(
            w1.at[:, 8 * k + l // 2], z3.at[pl.ds(6 * c + 3 * h, 3), g % 4],
            z2s.at[8 * k + l // 2], z2r.at[8 * c + r % 8], row=k, col=l
        )

    def second_from(k, l):
        return remote(
            w1.at[:, 8 * r + c // 2], z3.at[pl.ds(6 * l + 3 * (k % 2), 3), k // 2 % 4],
            z2s.at[8 * r + c // 2], z2r.at[8 * l + k % 8], row=k, col=l
        )

    def here2():
        return pltpu.make_async_copy(
            w1.at[:, 8 * r + c // 2], z3.at[pl.ds(6 * c + 3 * h, 3), g % 4], lsem.at[2]
        )

    def send_second(j):
        k = lax.rem(r + j, ROWS)

        def go(i):
            l = lax.rem(2 * i + c, COLS) // 2 * 2 + r // 8
            p = 8 * k + l // 2
            w1[:, p] = z1[:, maps_ref[s, p]]

            @pl.when((k == r) & (l == c))
            def _():
                here2().start()

            @pl.when(jnp.logical_not((k == r) & (l == c)))
            def _():
                second(k, l).start()

        each(0, 8, go)

    each(1, 17, send_second)

    swap_back.wait_recv()
    for p in range(3):
        for q in range(p + 1):
            total = pivot_ref[128 * p:128 * (p + 1), 128 * q:128 * (q + 1)].astype(F32)
            for child in range(2):
                i, j = maps_ref[child, p], maps_ref[child, q]
                present = (i < 3) & (j < 3)
                i, j = jnp.minimum(i, 2), jnp.minimum(j, 2)
                block = crn[child, :, i * (i + 1) // 2 + j].astype(F32).reshape(128, 128)
                total = total + jnp.where(present, block, 0.0)
            a_ref[128 * p:128 * (p + 1), 128 * q:128 * (q + 1)] = total
    factor_inverse(a_ref, parent_inv, s_ref, i_ref, l_ref)

    @pl.when(keeps)
    def _():
        here2().wait()

    def not_self(k, l):
        return jnp.logical_not((k == r) & (l == c))

    def pivots_rest(j):
        k = 8 * (c % 2) + 2 * j

        @pl.when(not_self(k, 0))
        def _():
            second_from(k, 0).wait_recv()

    each(0, 4, pivots_rest)
    for p in range(3):
        zf[p] = z3[p]
    for p in range(3):
        fs[p] = zf[jnp.minimum(maps_ref[s, p], 3)]
    swap_pivots = remote(fs, fr, sws.at[1], swr.at[1], sib=other)
    swap_pivots.start()
    swap_pivots.wait_recv()
    first_rows = (r == 0) & (c < 6)
    start_row = pl.multiple_of(64 * jnp.minimum(c, 5), 64)
    anchor = jnp.where(first_rows, pivot_ref[pl.ds(start_row, 64), :].astype(F32), 0.0)
    rows = jnp.concatenate(
        [fs[p].astype(F32).reshape(64, 128) + fr[p].astype(F32).reshape(64, 128) for p in range(3)], axis=1
    )
    piece = mm_nt(rows + anchor, parent_inv[...]).astype(BF16)
    prow[c] = piece

    mine = pl.ds(pl.multiple_of(32 * s, 32), 32)
    theirs = pl.ds(pl.multiple_of(32 * other, 32), 32)

    def gather_rows(k):
        return remote(prow.at[c, mine], prow.at[c, mine], g1s.at[k], g1r.at[c], col=k)

    def gather_rows_from(k):
        return remote(prow.at[c, mine], prow.at[k, mine], g1s.at[k], g1r.at[k], col=k)

    def hand_rows(k):
        return remote(prow.at[k, mine], prow.at[k, mine], hs.at[k], hr.at[k], sib=other)

    def hand_rows_from(k):
        return remote(prow.at[k, mine], prow.at[k, theirs], hs.at[k], hr.at[k], sib=other)

    def gather_cols(k):
        return remote(prow.at[c], pcol.at[c % 8], g2s.at[k], g2r.at[c % 8], row=k, col=cols_to)

    def gather_cols_from(k):
        return remote(
            prow.at[c], pcol.at[k], g2s.at[k], g2r.at[k], row=cols_from_row, col=cols_from_col + k
        )

    def is_other(k):
        return jnp.logical_not((k == r) & (cols_to == c))

    @pl.when(sends_cols)
    def _():
        def go(j):
            k = lax.rem(r + j, ROWS)

            @pl.when(is_other(k))
            def _():
                gather_cols(k).start()

            @pl.when(jnp.logical_not(is_other(k)))
            def _():
                pcol[c % 8] = piece

        each(1, 17, go)

    each(1, 16, lambda j: gather_rows(lax.rem(c + j, COLS)).start())

    def second_rest(j):
        k, l = 8 * (c % 2) + j % 8, j // 8

        @pl.when(not_self(k, l) & ((l > 0) | (k % 2 == 1)))
        def _():
            second_from(k, l).wait_recv()

    each(0, 128, second_rest)

    def strip(p):
        return z3[maps_ref[s, p]]

    def half(k):
        return remote(xs.at[pl.ds(4 * k, 4)], xr.at[pl.ds(4 * k, 4)], xss.at[k], xsr.at[k], sib=other)

    def send_half(j):
        k = lax.rem(c + j, COLS)
        for q in range(4):
            xs[4 * k + q] = strip(64 * other + 4 * k + q)
        half(k).start()

    each(1, 17, send_half)

    def fourth(k):
        return remote(y.at[pl.ds(4 * k, 4)], z4.at[c], z4s.at[k], z4r.at[c], col=k)

    def fourth_from(k):
        return remote(y.at[pl.ds(4 * k, 4)], z4.at[k], z4s.at[k], z4r.at[k], col=k)

    def both(k, q):
        return (strip(64 * s + 4 * k + q).astype(F32) + xr[4 * k + q].astype(F32)).astype(BF16)

    def send_fourth(j):
        k = lax.rem(c + j, COLS)
        half(k).wait_recv()
        for q in range(4):
            y[4 * k + q] = both(k, q)
        fourth(k).start()

    each(1, 16, send_fourth)
    half(c).wait_recv()
    for q in range(4):
        z4[c, q] = both(c, q)

    def cols_rest(k):
        @pl.when(jnp.logical_not((cols_from_row == r) & (cols_from_col + k == c)))
        def _():
            gather_cols_from(k).wait_recv()

    each(0, 8, cols_rest)

    def hand(j):
        k = lax.rem(c + COLS - j, COLS)
        gather_rows_from(k).wait_recv()
        hand_rows(k).start()

    each(1, 16, hand)
    for chunk in range(4):
        def rows_rest(k):
            @pl.when(k != c)
            def _():
                hand_rows_from(k).wait_recv()
                fourth_from(k).wait_recv()

        each(4 * chunk, 4 * chunk + 4, rows_rest)
        left = prow[4 * chunk:4 * chunk + 4].reshape(256, 384)
        panel_ref[256 * chunk:256 * (chunk + 1), :] = left
        row_ids = 1024 * r + 256 * chunk + lax.broadcasted_iota(jnp.int32, (256, 128), 0)
        for q in range(4):
            right = pcol[2 * q:2 * q + 2].reshape(128, 384)
            front = z4[4 * chunk:4 * chunk + 4, q].astype(F32).reshape(256, 128)
            value = front - dot_nt(left, right)
            col_ids = 512 * (16 * s + c) + 128 * q + lax.broadcasted_iota(jnp.int32, (256, 128), 1)
            value = jnp.where((row_ids >= 384) & (col_ids >= 384), value, 0.0)
            update_ref[256 * chunk:256 * (chunk + 1), 128 * q:128 * (q + 1)] = value.astype(BF16)

    @pl.when(is_root)
    def _():
        each(1, 16, lambda j: scatter(lax.rem(r + j, ROWS)).wait_send())

    to_others(lambda k: spread(k).wait_send())

    @pl.when(at_root)
    def _():
        each(1, 8, lambda k: corner_a(k).wait_send())

    @pl.when(holds & (c == 0))
    def _():
        each(1, 16, lambda k: corner_b(k).wait_send())

    @pl.when(holds)
    def _():
        each(1, 16, lambda j: corner_c(lax.rem(r + j, ROWS)).wait_send())

    @pl.when(sends_cols)
    def _():
        def gone(k):
            @pl.when(is_other(k))
            def _():
                gather_cols(k).wait_send()

        each(0, 16, gone)

    def all_gone(j):
        k = lax.rem(r + j, ROWS)
        first(k).wait_send()
        k = lax.rem(c + j, COLS)
        fourth(k).wait_send()
        gather_rows(k).wait_send()
        hand_rows(k).wait_send()

    each(1, 16, all_gone)

    def second_gone(j):
        k, l = j // 8, 2 * (j % 8) + r // 8

        @pl.when(jnp.logical_not((k == r) & (l == c)))
        def _():
            second(k, l).wait_send()

    each(0, 128, second_gone)
    each(0, 16, lambda k: half(k).wait_send())
    swap.wait_send()
    swap_pivots.wait_send()


def front_step(maps, trailing, border, child, pivot):
    vmem = pl.BlockSpec(memory_space=pltpu.VMEM)
    dma = pltpu.SemaphoreType.DMA
    buffers = [
        (16, 48, 384),
        (768, 384), (768, 384),
        (6, 6, 8, 16, 128),
        (8, 6, 16, 128),
        (3, 97, 16, 128),
        (3, 128, 16, 128),
        (97, 4, 16, 128),
        (4, 4, 16, 128),
        (64, 4, 16, 128), (64, 4, 16, 128),
        (3, 4, 16, 128), (3, 4, 16, 128),
        (64, 4, 16, 128),
        (16, 4, 4, 16, 128),
        (16, 64, 384), (8, 64, 384),
        (2, 8, 6, 16, 128),
    ]
    counts = [16, 1] + [16] * 4 + [128] * 2 + [16] * 6 + [8, 1, 16, 1, 16, 8, 2, 2, 16, 16, 16, 16, 5]
    return pl.pallas_call(
        front_kernel,
        out_shape=(
            jax.ShapeDtypeStruct((1024, 384), BF16),
            jax.ShapeDtypeStruct((1024, 512), BF16),
        ),
        in_specs=[pl.BlockSpec(memory_space=pltpu.SMEM)] + [vmem] * 4,
        out_specs=(vmem, vmem),
        scratch_shapes=[pltpu.VMEM(shape, BF16) for shape in buffers]
        + [pltpu.VMEM((384, 384), F32)]
        + FACTOR_SCRATCH
        + [dma((count,)) for count in counts]
        + [pltpu.SemaphoreType.REGULAR],
        compiler_params=pltpu.CompilerParams(
            collective_id=0, has_side_effects=True, vmem_limit_bytes=50 << 20
        ),
        cost_estimate=pl.CostEstimate(flops=10**10, bytes_accessed=10**8, transcendentals=0),
    )(maps, trailing, border, child, pivot)


def inverse_maps(child_maps):
    matches = child_maps[:, :, None] == jnp.arange(128, dtype=jnp.int32)
    source = jnp.arange(96, dtype=jnp.int32)[None, :, None]
    return jnp.min(jnp.where(matches, source, 96), axis=1).astype(jnp.int32)


def shards(child_pivot, child_border, child_trailing, parent_pivot, child_maps):
    border = child_border[0].reshape(16, 48, 384)
    return front_step(inverse_maps(child_maps), child_trailing[0], border, child_pivot[0], parent_pivot)


def solution(mesh):
    placed = (P("sib", None, None), P("sib", "row", None), P("sib", "row", "col"), P(), P())
    return jax.shard_map(
        shards,
        mesh=mesh,
        in_specs=placed,
        out_specs=(P("row", None), P("row", ("sib", "col"))),
        check_vma=False,
    )
```
